32 devices in a mesh: seq: 8 (over y, x, core), dp: 4 (over z).
Axes of the slice: x: 2, y: 2, z: 4, core: 2. Of those that a mesh axis runs over, the one named last changes fastest.
Arguments:
- queries: bfloat16 [4, 2048, 2048], P('dp', 'seq'), may hold values from -32 to 32
- keys: bfloat16 [4, 2048, 2048], P('dp', 'seq'), may hold values from -9 to 9
- values: bfloat16 [4, 2048, 2048], P('dp', 'seq'), may hold values from -6 to 6
- out_grad: bfloat16 [4, 2048, 2048], P('dp', 'seq'), may hold values from -6 to 6
- adjacency: int32 [4, 16, 8], P('dp', 'seq'), may hold values from 0 to 15, as said below
- counts: int32 [4, 16], P('dp', 'seq'), may hold values from 1 to 8, as said below
- sink: float32 [16], replicated, may hold values from 4 to 10
Outputs:
- attended: bfloat16 [4, 2048, 2048], P('dp', 'seq')
- query_grad: bfloat16 [4, 2048, 2048], P('dp', 'seq')
- key_grad: bfloat16 [4, 2048, 2048], P('dp', 'seq')
- value_grad: bfloat16 [4, 2048, 2048], P('dp', 'seq')
- sink_grad: float32 [16], replicated
The draws below stay inside these ranges and needn't reach their ends.
Inputs may be any that keep to these rules, and one draw needn't show every extreme that they name: `adjacency`: row b of a sequence lists key blocks of the same sequence; slot 0 is b itself; the first counts[b] entries are distinct, and each lies on a device at most 2 seq indices from the device of block b (block c lies at seq index c // 2); entries after counts[b] equal b. `counts`: some block has 8 live entries.
All inputs are finite; a program needn't handle non-finite values.
Results may differ from the reference program's by a relative error of at most 0.014.
Values may be sent and summed in bfloat16 or wider, within the bound.
No kernel may reach another device: no remote copies, remote signals or barrier semaphores. Data moves between devices by JAX's collectives and lax.ppermute only.
A program may use at most 192 MiB of HBM per device.

```python
import jax
import jax.numpy as jnp
from jax import lax

H = 16
HD = 128
BLK = 128
RADIUS = 2
MAXADJ = 8
QB = 2
SEQS = 4
NBLK = 16
LEN = 2048


def block_lists(key):
    base = jax.random.fold_in(key, 7)
    rank_key, load_key, count_key = jax.random.split(base, 3)
    width = (2 * RADIUS + 1) * QB
    blocks = lax.broadcasted_iota(jnp.int32, (NBLK,), 0)
    device = blocks // QB
    start = (device - RADIUS) * QB
    spread = lax.broadcasted_iota(jnp.int32, (width,), 0)
    candidates = start[:, None] + spread[None, :]
    usable = (candidates >= 0) & (candidates < NBLK) & (candidates != blocks[:, None])
    ranking = jax.random.randint(rank_key, (SEQS, NBLK, width), 0, 1 << 20) * width + spread[None, None, :]
    ranking = jnp.where(usable[None, :, :], ranking, (1 << 30) + spread[None, None, :])
    order = jnp.argsort(ranking, axis=-1, stable=True)
    widened = jnp.broadcast_to(candidates[None, :, :], (SEQS, NBLK, width))
    picked = jnp.take_along_axis(widened, order, axis=-1)[:, :, :MAXADJ - 1]
    usable_count = jnp.sum(usable.astype(jnp.int32), axis=1)
    loads = jax.random.randint(load_key, (SEQS, NBLK // QB), 1, MAXADJ + 1)
    device_load = jnp.take(loads, device, axis=1)
    live = 1 + jax.random.randint(count_key, (SEQS, NBLK), 0, 1 << 20) % device_load
    live = jnp.minimum(live, usable_count[None, :] + 1)
    live = live.at[:, NBLK // 2].set(MAXADJ)
    own_block = jnp.broadcast_to(blocks[None, :, None], (SEQS, NBLK, 1))
    slot_lists = jnp.concatenate([own_block, picked], axis=2)
    slot_number = lax.broadcasted_iota(jnp.int32, (SEQS, NBLK, MAXADJ), 2)
    slot_lists = jnp.where(slot_number < live[:, :, None], slot_lists, blocks[None, :, None])
    return (slot_lists.astype(jnp.int32), live.astype(jnp.int32))


def draw_adjacency(key, part):
    return block_lists(key)[0]


def draw_counts(key, part):
    return block_lists(key)[1]


def paired_fields(key):
    base = jax.random.fold_in(key, 11)
    first_key, second_key = jax.random.split(base, 2)
    shape = (SEQS, LEN, H * HD)
    query_field = 1.5 * jax.random.truncated_normal(first_key, -6.0, 6.0, shape, jnp.float32)
    key_field = 1.5 * jax.random.truncated_normal(second_key, -6.0, 6.0, shape, jnp.float32)
    return (query_field, key_field)


def draw_queries(key, part):
    return paired_fields(key)[0].astype(jnp.bfloat16)


def draw_keys(key, part):
    return paired_fields(key)[1].astype(jnp.bfloat16)


def steps_of(key, dims, cuts, low, high):
    gain = 1.0
    for position, parts in cuts:
        draws = jax.random.uniform(jax.random.fold_in(jax.random.fold_in(key, 6), position), (parts,), jnp.float32, low / len(cuts), high / len(cuts))
        gain = gain * jnp.repeat(jnp.exp(draws), dims[position] // parts).reshape((-1,) + (1,) * (len(dims) - 1 - position))
    return gain


def noise(key, shape, scale, bound, cuts=(), dtype=jnp.bfloat16):
    entries = jax.random.normal(key, shape, jnp.float32) * scale
    if len(cuts) > 0:
        entries = steps_of(key, shape, cuts, -0.22, 0.18) * entries
    return jnp.clip(entries, min=-bound, max=bound).astype(dtype)


def setup_inputs(seed: int = 0) -> dict:
    key_list = jax.random.split(jax.random.key(seed), 8)
    queries = draw_queries(jax.random.fold_in(key_list[7], 71), 0)
    keys = draw_keys(jax.random.fold_in(key_list[7], 71), 0)
    values = noise(key_list[2], (SEQS, LEN, H * HD), 1.0, 6.0, ((0, 4), (1, 8)))
    out_grad = noise(key_list[3], (SEQS, LEN, H * HD), 1.0, 6.0, ((0, 4), (1, 8)))
    adjacency = draw_adjacency(jax.random.fold_in(key_list[7], 71), 0)
    counts = draw_counts(jax.random.fold_in(key_list[7], 71), 0)
    sink = jnp.clip(jax.random.uniform(key_list[6], (H,), jnp.float32, 4.0, 10.0), 4.0, 10.0)
    return {"queries": queries, "keys": keys, "values": values, "out_grad": out_grad, "adjacency": adjacency, "counts": counts, "sink": sink}


def reference(queries, keys, values, out_grad, adjacency, counts, sink):
    score_scale = HD ** -0.5
    block_count = LEN // BLK
    sink_col = sink[:, None]

    def one_sequence(sink_sum, items):
        query_seq, key_seq, value_seq, grad_seq, slot_lists, live_count = items
        query_all = query_seq.reshape(block_count, BLK, H, HD).astype(jnp.float32)
        key_all = key_seq.reshape(block_count, BLK, H, HD).astype(jnp.float32)
        value_all = value_seq.reshape(block_count, BLK, H, HD).astype(jnp.float32)
        grad_all = grad_seq.reshape(block_count, BLK, H, HD).astype(jnp.float32)

        def one_block(grads_pair, block_items):
            key_grads, value_grads = grads_pair
            query_blk, grad_blk, slot_row, live_num = block_items
            key_slots = key_all[slot_row]
            value_slots = value_all[slot_row]
            live_slot = lax.broadcasted_iota(jnp.int32, (MAXADJ,), 0) < live_num
            scores = jnp.einsum("qhd,jkhd->hqjk", query_blk, key_slots) * score_scale
            scores = jnp.where(live_slot[None, None, :, None], scores, -jnp.inf)
            row_max = jnp.maximum(jnp.max(scores, axis=(2, 3)), sink_col)
            powers = jnp.exp(scores - row_max[:, :, None, None])
            row_total = jnp.sum(powers, axis=(2, 3)) + jnp.exp(sink_col - row_max)
            probs = powers / row_total[:, :, None, None]
            probs_low = lax.optimization_barrier(probs.astype(jnp.bfloat16)).astype(jnp.float32)
            attended = jnp.einsum("hqjk,jkhd->qhd", probs_low, value_slots)
            attended_low = lax.optimization_barrier(attended.astype(jnp.bfloat16))
            row_delta = jnp.einsum("qhd,qhd->hq", grad_blk, attended_low.astype(jnp.float32))
            dprobs = jnp.einsum("qhd,jkhd->hqjk", grad_blk, value_slots)
            dscores = (probs * (dprobs - row_delta[:, :, None, None])).astype(jnp.bfloat16)
            dscores_wide = lax.optimization_barrier(dscores).astype(jnp.float32)
            query_grad = jnp.einsum("hqjk,jkhd->qhd", dscores_wide, key_slots) * score_scale
            key_terms = jnp.einsum("hqjk,qhd->jkhd", dscores_wide, query_blk) * score_scale
            value_terms = jnp.einsum("hqjk,qhd->jkhd", probs_low, grad_blk)
            key_grads = key_grads.at[slot_row].add(key_terms)
            value_grads = value_grads.at[slot_row].add(value_terms)
            sink_prob = jnp.exp(sink_col - row_max) / row_total
            sink_term = -jnp.sum(sink_prob * row_delta, axis=1)
            return (key_grads, value_grads), (attended_low, query_grad.astype(jnp.bfloat16), sink_term)

        zero_grads = jnp.zeros((block_count, BLK, H, HD), jnp.float32)
        grads_pair, block_outs = lax.scan(one_block, (zero_grads, zero_grads), (query_all, grad_all, slot_lists, live_count))
        attended_seq = block_outs[0].reshape(LEN, H * HD)
        query_seq_grad = block_outs[1].reshape(LEN, H * HD)
        key_seq_grad = grads_pair[0].astype(jnp.bfloat16).reshape(LEN, H * HD)
        value_seq_grad = grads_pair[1].astype(jnp.bfloat16).reshape(LEN, H * HD)
        sink_sum = sink_sum + jnp.sum(block_outs[2], axis=0)
        return sink_sum, (attended_seq, query_seq_grad, key_seq_grad, value_seq_grad)

    sink_grad, outputs = lax.scan(one_sequence, jnp.zeros((H,), jnp.float32), (queries, keys, values, out_grad, adjacency, counts))
    return outputs[0], outputs[1], outputs[2], outputs[3], sink_grad
```

```python
import functools

import jax
import jax.numpy as jnp
from jax import lax
from jax.experimental import pallas as pl
from jax.experimental.pallas import tpu as pltpu
from jax.sharding import PartitionSpec as P

HD = 128
BLK = 128
RADIUS = 2
GROUP = 8
NOTE = 16
LOG2E = 1.4426950408889634
VMEM_LIMIT = 48 * 1024 * 1024
NT = (((1,), (1,)), ((), ()))
NN = (((1,), (0,)), ((), ()))
ANY = pl.BlockSpec(memory_space=pl.ANY)
SMEM = pl.BlockSpec(memory_space=pltpu.SMEM)
VMEM = pl.BlockSpec(memory_space=pltpu.VMEM)


def sending_order(group):
    return sorted(range(group), key=lambda k: (k & 2 == 0, k & 4 == 0, k == 0))


def pack_kernel(group, per_device, head, adjacency, counts, *refs):
    sources, parcels = refs[:4], refs[4 : 4 + group]
    stage, note, in_sems, out_sems = refs[4 + group :]
    tokens = sources[0].shape[1]
    rank = lax.axis_index("seq")
    spot = lax.rem(rank, group)
    order = sending_order(group)
    reads = {}
    for k in order:
        column = pl.multiple_of(((spot ^ k) * per_device + head) * HD, HD)
        for a, source in enumerate(sources):
            reads[k, a] = pltpu.make_async_copy(
                source.at[0, :, pl.ds(column, HD)],
                stage.at[k, pl.ds(a * tokens, tokens)],
                in_sems.at[k, a],
            )
            reads[k, a].start()
    own_blocks, slots = adjacency.shape[1:]
    rows = lax.broadcasted_iota(jnp.int32, note.shape, 0)
    lanes = lax.broadcasted_iota(jnp.int32, note.shape, 1)
    marks = jnp.zeros(note.shape, jnp.int32)
    for b in range(own_blocks):
        for j in range(slots):
            marks = jnp.where(
                (rows == b) & (lanes == j), adjacency[0, b, j] - rank * own_blocks, marks
            )
        marks = jnp.where((rows == b) & (lanes == slots), counts[0, b], marks)
    note[...] = marks.astype(jnp.float32)
    for k in range(group):
        stage[k, 4 * tokens :, :] = note[...].astype(jnp.bfloat16)
    writes = []
    for k in order:
        for a in range(4):
            reads[k, a].wait()
        writes.append(pltpu.make_async_copy(stage.at[k], parcels[k], out_sems.at[k]))
        writes[-1].start()
    for write in writes:
        write.wait()


def pack(adjacency, counts, sources, group, per_device, head):
    tokens = sources[0].shape[1]
    rows = 4 * tokens + NOTE
    return pl.pallas_call(
        functools.partial(pack_kernel, group, per_device, head),
        out_shape=[jax.ShapeDtypeStruct((rows, HD), jnp.bfloat16)] * group,
        in_specs=[SMEM] * 2 + [ANY] * 4,
        out_specs=[ANY] * group,
        scratch_shapes=[
            pltpu.VMEM((group, rows, HD), jnp.bfloat16),
            pltpu.VMEM((NOTE, HD), jnp.float32),
            pltpu.SemaphoreType.DMA((group, 4)),
            pltpu.SemaphoreType.DMA((group,)),
        ],
        compiler_params=pltpu.CompilerParams(vmem_limit_bytes=VMEM_LIMIT),
        cost_estimate=pl.CostEstimate(
            flops=0, bytes_accessed=group * rows * HD * 4, transcendentals=0
        ),
        name="pack",
    )(adjacency, counts, *sources)


def unpack_kernel(group, per_device, head, *refs):
    parcels, outs = refs[:group], refs[-7:-3]
    stage, in_sems, out_sems = refs[-3:]
    tokens = outs[0].shape[1]
    spot = lax.rem(lax.axis_index("seq"), group)
    reads = []
    for k in range(group):
        reads.append(pltpu.make_async_copy(parcels[k], stage.at[k], in_sems.at[k]))
        reads[-1].start()
    writes = []
    for k in range(group):
        column = pl.multiple_of(((spot ^ k) * per_device + head) * HD, HD)
        reads[k].wait()
        for a, out in enumerate(outs):
            writes.append(
                pltpu.make_async_copy(
                    stage.at[k, pl.ds(a * tokens, tokens)],
                    out.at[0, :, pl.ds(column, HD)],
                    out_sems.at[k, a],
                )
            )
            writes[-1].start()
    for write in writes:
        write.wait()


def unpack(parcels, outs, group, per_device, head):
    rows = parcels[0].shape[0]
    shape = jax.ShapeDtypeStruct((1, rows // 4, group * per_device * HD), jnp.bfloat16)
    held = [] if outs is None else list(outs)
    return pl.pallas_call(
        functools.partial(unpack_kernel, group, per_device, head),
        out_shape=[shape] * 4,
        in_specs=[ANY] * (group + len(held)),
        out_specs=[ANY] * 4,
        scratch_shapes=[
            pltpu.VMEM((group, rows, HD), jnp.bfloat16),
            pltpu.SemaphoreType.DMA((group,)),
            pltpu.SemaphoreType.DMA((group, 4)),
        ],
        input_output_aliases={group + a: a for a in range(len(held))},
        compiler_params=pltpu.CompilerParams(vmem_limit_bytes=VMEM_LIMIT),
        cost_estimate=pl.CostEstimate(
            flops=0, bytes_accessed=group * rows * HD * 4, transcendentals=0
        ),
        name="unpack",
    )(*parcels, *held)


def attend_kernel(group, per_device, head, halo, slots, own_blocks, scale, *refs):
    sink, sink_in = refs[:2]
    parcels = refs[2 : 2 + group]
    refs = refs[2 + group :]
    if halo:
        halo_in, refs = refs[0], refs[1:]
    results, sink_out = refs[:group], refs[group]
    refs = refs[group + 1 :]
    if halo:
        halo_out, refs = refs[0], refs[1:]
    kv, qd, notes, marks, lists, kt, vt, diag, diag_back, scored, paired, acc, out = refs[:13]
    sink_acc, sems, list_sem, out_sems = refs[13:]

    blocks = own_blocks * group
    span = own_blocks * BLK
    edge = halo * BLK
    window = blocks + 2 * halo
    spot = lax.rem(lax.axis_index("seq"), group)
    number = spot * per_device + head
    note_copies, copies = [], []
    for k in range(group):
        other = spot ^ k
        note_copies.append(
            pltpu.make_async_copy(
                parcels[k].at[pl.ds(4 * span, NOTE)], notes.at[other], sems.at[k, 4]
            )
        )
    for k in range(group):
        row = pl.multiple_of((spot ^ k) * span, span)
        targets = (
            kv.at[pl.ds(row + edge, span), pl.ds(0, HD)],
            kv.at[pl.ds(row + edge, span), pl.ds(HD, HD)],
            qd.at[pl.ds(row, span), pl.ds(0, HD)],
            qd.at[pl.ds(row, span), pl.ds(HD, HD)],
        )
        for a, target in enumerate(targets):
            copies.append(
                pltpu.make_async_copy(parcels[k].at[pl.ds(a * span, span)], target, sems.at[k, a])
            )
    if halo:
        copies.append(pltpu.make_async_copy(halo_in.at[0], kv.at[pl.ds(0, edge)], sems.at[group, 0]))
        copies.append(
            pltpu.make_async_copy(
                halo_in.at[1], kv.at[pl.ds(edge + blocks * BLK, edge)], sems.at[group, 1]
            )
        )
    for copy in note_copies + copies:
        copy.start()
    diag[...] = jnp.zeros_like(diag)
    diag_back[...] = jnp.zeros_like(diag_back)
    acc[...] = jnp.zeros_like(acc)
    sink_acc[...] = jnp.zeros_like(sink_acc)
    for copy in note_copies:
        copy.wait()
    for j in range(group):
        marks[pl.ds(j * own_blocks, own_blocks), :] = (
            notes[j].astype(jnp.float32).astype(jnp.int32)[:own_blocks]
        )
    list_copy = pltpu.make_async_copy(marks, lists, list_sem)
    list_copy.start()
    for copy in copies:
        copy.wait()

    def turn(c, carry):
        rows = kv[pl.ds(pl.multiple_of(c * BLK, BLK), BLK), :]
        kt[c] = rows[:, :HD].T
        vt[c] = rows[:, HD:].T
        return carry

    lax.fori_loop(0, window, turn, 0)
    list_copy.wait()

    to_log2 = scale * LOG2E
    sink_log2 = sink[number] * LOG2E

    def folded(x, op):
        return functools.reduce(op, [x[r : r + 8] for r in range(0, x.shape[0], 8)])

    def one_block(b, carry):
        rows = pl.ds(pl.multiple_of(b * BLK, BLK), BLK)
        home = b // own_blocks * own_blocks + halo
        query = qd[rows, :HD]
        grad = qd[rows, HD:]
        diag[:BLK, :HD] = query
        diag[BLK:, HD:] = grad
        diag_back[:BLK, :HD] = grad
        diag_back[BLK:, HD:] = query

        def with_slots(live):
            at = [lists[b, j] + home for j in range(live)]
            key_rows = [pl.ds(pl.multiple_of(c * BLK, BLK), BLK) for c in at]
            weights = diag[...]
            top = None
            for j in range(live):
                both = lax.dot_general(kv[key_rows[j], :], weights, NT, preferred_element_type=jnp.float32)
                scored[j] = both
                part = folded(both[:, :BLK], jnp.maximum)
                top = part if top is None else jnp.maximum(top, part)
            top = jnp.maximum(jnp.max(top, axis=0, keepdims=True) * to_log2, sink_log2)
            total = jnp.zeros((8, BLK), jnp.float32)
            dotted = jnp.zeros((8, BLK), jnp.float32)
            for j in range(live):
                power = jnp.exp2(scored[j, :, :BLK] * to_log2 - top)
                scored[j, :, :BLK] = power
                total = total + folded(power, jnp.add)
                dotted = dotted + folded(power * scored[j, :, BLK:], jnp.add)
            sink_power = jnp.exp2(sink_log2 - top)
            inverse = 1.0 / (jnp.sum(total, axis=0, keepdims=True) + sink_power)
            delta = jnp.sum(dotted, axis=0, keepdims=True) * inverse
            sink_acc[...] += sink_power * inverse * delta
            weights = diag_back[...]
            for j in range(live):
                probs = scored[j, :, :BLK] * inverse
                dscores = probs * (scored[j, :, BLK:] - delta)
                pair = jnp.concatenate([probs, dscores], axis=1).astype(jnp.bfloat16)
                paired[pl.ds(j * BLK, BLK), :] = pair
                acc[key_rows[j], :] += lax.dot_general(
                    pair, weights, NN, preferred_element_type=jnp.float32
                )
            attended = lax.dot_general(
                jnp.concatenate([vt[c] for c in at], axis=1),
                paired[: live * BLK, :BLK],
                NN,
                preferred_element_type=jnp.float32,
            )
            query_grad = lax.dot_general(
                jnp.concatenate([kt[c] for c in at], axis=1),
                paired[: live * BLK, BLK:],
                NN,
                preferred_element_type=jnp.float32,
            )
            out[2, rows, :] = attended.astype(jnp.bfloat16).T
            out[3, rows, :] = (query_grad * scale).astype(jnp.bfloat16).T

        for live in range(1, slots + 1):
            pl.when(lists[b, slots] == live)(functools.partial(with_slots, live))
        return carry

    lax.fori_loop(0, blocks, one_block, 0)

    def finish(b, carry):
        rows = pl.ds(pl.multiple_of(b * BLK, BLK), BLK)
        from_rows = pl.ds(pl.multiple_of((b + halo) * BLK, BLK), BLK)
        out[0, rows, :] = acc[from_rows, :HD].astype(jnp.bfloat16)
        out[1, rows, :] = (acc[from_rows, HD:] * scale).astype(jnp.bfloat16)
        return carry

    lax.fori_loop(0, blocks, finish, 0)
    lanes = lax.broadcasted_iota(jnp.int32, (1, BLK), 1)
    sink_sum = jnp.sum(sink_acc[...], axis=1, keepdims=True)
    sink_out[...] = sink_in[...] - jnp.where(lanes == number, sink_sum, 0.0)
    copies = []
    for k in sending_order(group):
        row = pl.multiple_of((spot ^ k) * span, span)
        for a in range(4):
            copies.append(
                pltpu.make_async_copy(
                    out.at[a, pl.ds(row, span)],
                    results[k].at[pl.ds(a * span, span)],
                    out_sems.at[k, a],
                )
            )
    for copy in copies:
        copy.start()
    if halo:
        for side, row in ((0, 0), (1, edge + blocks * BLK)):
            halo_out[side, :, :HD] = acc[pl.ds(row, edge), :HD]
            halo_out[side, :, HD:] = acc[pl.ds(row, edge), HD:] * scale
    for copy in copies:
        copy.wait()


def attend(sink, sink_in, parcels, halo_in, group, per_device, head, halo, slots, own_blocks, scale):
    span = own_blocks * BLK
    edge = halo * BLK
    blocks = own_blocks * group
    window = blocks + 2 * halo
    out_shape = [jax.ShapeDtypeStruct((4 * span, HD), jnp.bfloat16)] * group
    out_shape.append(jax.ShapeDtypeStruct((1, BLK), jnp.float32))
    out_specs = [ANY] * group + [VMEM]
    extra = []
    if halo:
        extra = [halo_in]
        out_shape.append(jax.ShapeDtypeStruct((2, edge, 2 * HD), jnp.float32))
        out_specs.append(VMEM)
    work = blocks * 4
    return pl.pallas_call(
        functools.partial(attend_kernel, group, per_device, head, halo, slots, own_blocks, scale),
        out_shape=out_shape,
        in_specs=[SMEM, VMEM] + [ANY] * (group + len(extra)),
        out_specs=out_specs,
        scratch_shapes=[
            pltpu.VMEM((window * BLK, 2 * HD), jnp.bfloat16),
            pltpu.VMEM((blocks * BLK, 2 * HD), jnp.bfloat16),
            pltpu.VMEM((group, NOTE, HD), jnp.bfloat16),
            pltpu.VMEM((blocks, HD), jnp.int32),
            pltpu.SMEM((blocks, HD), jnp.int32),
            pltpu.VMEM((window, HD, BLK), jnp.bfloat16),
            pltpu.VMEM((window, HD, BLK), jnp.bfloat16),
            pltpu.VMEM((2 * BLK, 2 * HD), jnp.bfloat16),
            pltpu.VMEM((2 * BLK, 2 * HD), jnp.bfloat16),
            pltpu.VMEM((slots, BLK, 2 * BLK), jnp.float32),
            pltpu.VMEM((slots * BLK, 2 * BLK), jnp.bfloat16),
            pltpu.VMEM((window * BLK, 2 * HD), jnp.float32),
            pltpu.VMEM((4, blocks * BLK, HD), jnp.bfloat16),
            pltpu.VMEM((1, BLK), jnp.float32),
            pltpu.SemaphoreType.DMA((group + 1, 5)),
            pltpu.SemaphoreType.DMA,
            pltpu.SemaphoreType.DMA((group, 4)),
        ],
        compiler_params=pltpu.CompilerParams(vmem_limit_bytes=VMEM_LIMIT),
        cost_estimate=pl.CostEstimate(
            flops=work * 10 * BLK * BLK * HD,
            bytes_accessed=blocks * BLK * HD * 16,
            transcendentals=work * BLK * BLK,
        ),
        name="attend",
    )(sink, sink_in, *parcels, *extra)


def local(queries, keys, values, out_grad, adjacency, counts, sink):
    seq = lax.axis_size("seq")
    group = min(seq, GROUP)
    groups = seq // group
    heads = sink.shape[0]
    per_device = heads // group
    slots = adjacency.shape[2]
    own_blocks = adjacency.shape[1]
    span = own_blocks * BLK
    halo = RADIUS * own_blocks if groups > 1 else 0
    scale = HD ** (-0.5)
    spot = lax.rem(lax.axis_index("seq"), group)

    def swap(x, k, axis="seq"):
        if k == 0:
            return x
        return lax.ppermute(x, axis, [(i, i ^ k) for i in range(lax.axis_size(axis))])

    def beside(x, step):
        route = [(i, i + step * group) for i in range(seq) if 0 <= i + step * group < seq]
        return lax.ppermute(x, "seq", route)

    sources = (keys, values, queries, out_grad)
    arrived = []
    for head in range(per_device):
        parcels = pack(adjacency, counts, sources, group, per_device, head)
        moved = {k: swap(parcels[k], k) for k in sending_order(group)}
        arrived.append([moved[k] for k in range(group)])

    sink_row = jnp.zeros((1, BLK), jnp.float32)
    outs = None
    returned = []
    for head in range(per_device):
        parcels = arrived[head]
        halo_in = None
        if halo:
            stacked = jnp.stack(parcels)
            ends = []
            for side, step in ((group - RADIUS, 1), (0, -1)):
                near = [stacked[(side + r) ^ spot] for r in range(RADIUS)]
                near = [jnp.concatenate([x[:span], x[span : 2 * span]], axis=1) for x in near]
                ends.append(beside(jnp.concatenate(near, axis=0), step))
            halo_in = jnp.stack(ends)
        done = attend(
            sink, sink_row, parcels, halo_in, group, per_device, head, halo, slots, own_blocks, scale
        )
        results, sink_row = list(done[:group]), done[group]
        if halo:
            stacked = jnp.stack(results)
            for side, step, half in ((group - RADIUS, -1, 0), (0, 1, 1)):
                grads = beside(done[group + 1][half], step)
                for r in range(RADIUS):
                    at = (side + r) ^ spot
                    rows = stacked[at]
                    more = grads[r * span : (r + 1) * span]
                    more = jnp.concatenate([more[:, :HD], more[:, HD:]], axis=0)
                    wide = rows[: 2 * span].astype(jnp.float32) + more
                    rows = jnp.concatenate([wide.astype(jnp.bfloat16), rows[2 * span :]], axis=0)
                    stacked = lax.dynamic_update_index_in_dim(stacked, rows, at, 0)
            results = [stacked[k] for k in range(group)]
        moved = {k: swap(results[k], k) for k in sending_order(group)}
        returned.append([moved[k] for k in range(group)])
    for axis in ("dp", "seq"):
        step = 1
        while step < lax.axis_size(axis):
            sink_row = sink_row + swap(sink_row, step, axis)
            step *= 2
    for head in range(per_device):
        outs = unpack(returned[head], outs, group, per_device, head)
    value_grad, key_grad, attended, query_grad = outs
    return attended, query_grad, key_grad, value_grad, sink_row[0, :heads]


def solution(mesh):
    tokens = P("dp", "seq", None)
    return jax.shard_map(
        local,
        mesh=mesh,
        in_specs=(tokens, tokens, tokens, tokens, tokens, P("dp", "seq"), P()),
        out_specs=(tokens, tokens, tokens, tokens, P()),
        check_vma=False,
    )
```

```python
import functools

import jax
import jax.numpy as jnp
from jax import lax
from jax.experimental import pallas as pl
from jax.experimental.pallas import tpu as pltpu
from jax.sharding import PartitionSpec as P

HD = 128
BLK = 128
RADIUS = 2
GROUP = 8
NOTE = 16
LOG2E = 1.4426950408889634
VMEM_LIMIT = 48 * 1024 * 1024
NT = (((1,), (1,)), ((), ()))
NN = (((1,), (0,)), ((), ()))
ANY = pl.BlockSpec(memory_space=pl.ANY)
SMEM = pl.BlockSpec(memory_space=pltpu.SMEM)
VMEM = pl.BlockSpec(memory_space=pltpu.VMEM)
PARAMS = pltpu.CompilerParams(vmem_limit_bytes=VMEM_LIMIT)

DIRECT = {
    "steps": (0, 2, 3, 4, 5, 6),
    "rows": (1, 1, 1, 1, 1, 2, 2),
    "sent": ((0, 0), (6, 0), (1, 0), (2, 0), (3, 0), (4, 0), (5, 0), (6, 1)),
    "arrived": ((0, 0), (6, 0), (1, 0), (2, 0), (3, 0), (4, 0), (5, 0), (5, 1)),
    "merged": ((1, 5),),
}
PAIRED = {
    "steps": (0, 2, 4, 6),
    "rows": (1, 2, 2, 2, 4),
    "sent": ((0, 0), (4, 0), (1, 0), (4, 1), (2, 0), (4, 2), (3, 0), (4, 3)),
    "arrived": ((0, 0), (4, 0), (1, 0), (1, 1), (2, 0), (2, 1), (3, 0), (3, 1)),
    "merged": ((1, 1), (2, 2), (3, 3)),
}


def bytes_cost(count):
    return pl.CostEstimate(flops=0, bytes_accessed=count, transcendentals=0)


def run_copies(copies):
    for copy in copies:
        copy.start()
    for copy in copies:
        copy.wait()


def pack_kernel(group, per_device, head, tokens, layout, awaited, *refs):
    adjacency, counts = refs[:2]
    sources, outs = refs[2:6], refs[6 + awaited : -5]
    slots_here, counts_here, note, sems, list_sems = refs[-5:]
    rank = lax.axis_index("seq")
    spot = lax.rem(rank, group)
    copies = []
    for k in range(group):
        n, row = layout[k]
        column = pl.multiple_of(((spot ^ k) * per_device + head) * HD, HD)
        for a, source in enumerate(sources):
            copies.append(
                pltpu.make_async_copy(
                    source.at[0, :, pl.ds(column, HD)],
                    outs[n].at[pl.ds(row + a * tokens, tokens)],
                    sems.at[k, a],
                )
            )
    for copy in copies:
        copy.start()
    if head == 0:
        run_copies(
            (
                pltpu.make_async_copy(adjacency, slots_here, list_sems.at[0]),
                pltpu.make_async_copy(counts, counts_here, list_sems.at[1]),
            )
        )
        own_blocks, slots = adjacency.shape[1:]
        rows = lax.broadcasted_iota(jnp.int32, note.shape, 0)
        lanes = lax.broadcasted_iota(jnp.int32, note.shape, 1)
        marks = jnp.zeros(note.shape, jnp.int32)
        for b in range(own_blocks):
            for j in range(slots):
                near = slots_here[0, b, j] - rank * own_blocks
                marks = jnp.where((rows == b) & (lanes == j), near, marks)
            marks = jnp.where((rows == b) & (lanes == slots), counts_here[0, b], marks)
        note[...] = marks.astype(jnp.float32)
        for out in outs:
            row = out.shape[0] // (4 * tokens) * 4 * tokens
            out[row : row + NOTE, :] = note[...].astype(jnp.bfloat16)
    for copy in copies:
        copy.wait()


def pack(adjacency, counts, sources, awaited, route, group, per_device, head):
    tokens = sources[0].shape[1]
    size = 4 * tokens
    layout = [(n, row * size) for n, row in route["sent"]]
    rows = [n * size for n in route["rows"]]
    if head == 0:
        rows = [n * (size + NOTE) for n in route["rows"][:-1]] + [rows[-1] + NOTE]
    return pl.pallas_call(
        functools.partial(
            pack_kernel, group, per_device, head, tokens, layout, len(awaited)
        ),
        out_shape=[jax.ShapeDtypeStruct((r, HD), jnp.bfloat16) for r in rows],
        in_specs=[ANY] * (6 + len(awaited)),
        out_specs=[VMEM] * len(rows),
        scratch_shapes=[
            pltpu.SMEM(adjacency.shape, jnp.int32),
            pltpu.SMEM(counts.shape, jnp.int32),
            pltpu.VMEM((NOTE, HD), jnp.float32),
            pltpu.SemaphoreType.DMA((group, 4)),
            pltpu.SemaphoreType.DMA((2,)),
        ],
        compiler_params=PARAMS,
        cost_estimate=bytes_cost(group * size * HD * 4),
        name="pack",
    )(adjacency, counts, *sources, *awaited)


def pass_kernel(*refs):
    pass


def after(awaited, arrays):
    return pl.pallas_call(
        pass_kernel,
        out_shape=[jax.ShapeDtypeStruct(x.shape, x.dtype) for x in arrays],
        in_specs=[ANY] * (len(arrays) + len(awaited)),
        out_specs=[ANY] * len(arrays),
        input_output_aliases={n: n for n in range(len(arrays))},
        compiler_params=PARAMS,
        cost_estimate=bytes_cost(0),
        name="after",
    )(*arrays, *awaited)


def merge_kernel(moves, *refs):
    swapped, outs, sems = refs[0], refs[-1 - len(moves) : -1], refs[-1]
    copies = []
    for n, parts in enumerate(moves):
        for i, (row, to, count) in enumerate(parts):
            copies.append(
                pltpu.make_async_copy(
                    swapped.at[pl.ds(row, count)], outs[n].at[pl.ds(to, count)], sems.at[n, i]
                )
            )
    run_copies(copies)


def merge(swapped, buffers, route, size):
    buffers = list(buffers)
    noted = swapped.shape[0] % size != 0
    moves = []
    for row, _ in route["merged"]:
        parts = [(row * size, size, size)]
        if noted:
            parts.append((route["rows"][-1] * size, 2 * size + NOTE, NOTE))
        moves.append(parts)
    held = [buffers[n] for _, n in route["merged"]]
    filled = pl.pallas_call(
        functools.partial(merge_kernel, moves),
        out_shape=[jax.ShapeDtypeStruct(x.shape, x.dtype) for x in held],
        in_specs=[VMEM] + [ANY] * len(held),
        out_specs=[ANY] * len(held),
        scratch_shapes=[pltpu.SemaphoreType.DMA((len(held), 2))],
        input_output_aliases={1 + n: n for n in range(len(held))},
        compiler_params=PARAMS,
        cost_estimate=bytes_cost(len(held) * size * HD * 4),
        name="merge",
    )(swapped, *held)
    for (_, n), x in zip(route["merged"], filled):
        buffers[n] = x
    return buffers


def unpack_kernel(group, per_device, head, tokens, count, layout, *refs):
    parcels, outs, sems = refs[:count], refs[-5:-1], refs[-1]
    spot = lax.rem(lax.axis_index("seq"), group)
    copies = []
    for k, (n, from_row) in enumerate(layout):
        column = pl.multiple_of(((spot ^ k) * per_device + head) * HD, HD)
        for a, out in enumerate(outs):
            copies.append(
                pltpu.make_async_copy(
                    parcels[n].at[pl.ds(from_row + a * tokens, tokens)],
                    out.at[0, :, pl.ds(column, HD)],
                    sems.at[k, a],
                )
            )
    run_copies(copies)


def unpack(parcels, outs, route, group, per_device, head):
    count = len(parcels)
    tokens = parcels[0].shape[0] // 4
    layout = [(n, row * 4 * tokens) for n, row in route["arrived"]]
    shape = jax.ShapeDtypeStruct((1, tokens, group * per_device * HD), jnp.bfloat16)
    return pl.pallas_call(
        functools.partial(unpack_kernel, group, per_device, head, tokens, count, layout),
        out_shape=[shape] * 4,
        in_specs=[VMEM] * count + [ANY] * len(outs),
        out_specs=[ANY] * 4,
        scratch_shapes=[pltpu.SemaphoreType.DMA((group, 4))],
        input_output_aliases={count + a: a for a in range(len(outs))},
        compiler_params=PARAMS,
        cost_estimate=bytes_cost(group * tokens * HD * 16),
        name="unpack",
    )(*parcels, *outs)


def attend_kernel(group, per_device, head, halo, slots, own_blocks, scale, route, *refs):
    sink, sink_in, marks_in = refs[:3]
    arriving, leaving = route
    count = len(arriving["rows"])
    parcels, refs = refs[3 : 3 + count], refs[3 + count :]
    if halo:
        halo_in, refs = refs[0], refs[1:]
    count = len(leaving["rows"])
    results, sink_out, marks = refs[:count], refs[count], refs[count + 1]
    refs = refs[count + 2 :]
    if halo:
        halo_out, refs = refs[0], refs[1:]
    kv, qd, notes, lists, kt, vt, diag, diag_back, scored, paired, acc, out = refs[:12]
    sink_acc, sems, list_sem, out_sems = refs[12:]

    blocks = own_blocks * group
    span = own_blocks * BLK
    edge = halo * BLK
    window = blocks + 2 * halo
    spot = lax.rem(lax.axis_index("seq"), group)
    number = spot * per_device + head
    note_copies, copies = [], []
    for k, (n, row) in enumerate(arriving["arrived"] if head == 0 else ()):
        row = arriving["rows"][n] * 4 * span + row * NOTE
        note_copies.append(
            pltpu.make_async_copy(
                parcels[n].at[pl.ds(row, NOTE)], notes.at[spot ^ k], sems.at[k, 4]
            )
        )
    for k in range(group):
        row = pl.multiple_of((spot ^ k) * span, span)
        targets = (
            kv.at[pl.ds(row + edge, span), pl.ds(0, HD)],
            kv.at[pl.ds(row + edge, span), pl.ds(HD, HD)],
            qd.at[pl.ds(row, span), pl.ds(0, HD)],
            qd.at[pl.ds(row, span), pl.ds(HD, HD)],
        )
        n, part = arriving["arrived"][k]
        from_row = part * 4 * span
        for a, target in enumerate(targets):
            copies.append(
                pltpu.make_async_copy(
                    parcels[n].at[pl.ds(from_row + a * span, span)], target, sems.at[k, a]
                )
            )
    if halo:
        copies.append(pltpu.make_async_copy(halo_in.at[0], kv.at[pl.ds(0, edge)], sems.at[group, 0]))
        copies.append(
            pltpu.make_async_copy(
                halo_in.at[1], kv.at[pl.ds(edge + blocks * BLK, edge)], sems.at[group, 1]
            )
        )
    for copy in note_copies + copies:
        copy.start()
    diag[...] = jnp.zeros_like(diag)
    diag_back[...] = jnp.zeros_like(diag_back)
    acc[...] = jnp.zeros_like(acc)
    sink_acc[...] = jnp.zeros_like(sink_acc)
    for copy in note_copies:
        copy.wait()
    if head == 0:
        for j in range(group):
            marks[pl.ds(j * own_blocks, own_blocks), :] = (
                notes[j].astype(jnp.float32).astype(jnp.int32)[:own_blocks]
            )
    else:
        marks[...] = marks_in[...]
    list_copy = pltpu.make_async_copy(marks, lists, list_sem)
    list_copy.start()
    for copy in copies:
        copy.wait()

    def turn(c, carry):
        rows = kv[pl.ds(pl.multiple_of(c * BLK, BLK), BLK), :]
        kt[c] = rows[:, :HD].T
        vt[c] = rows[:, HD:].T
        return carry

    lax.fori_loop(0, window, turn, 0)
    list_copy.wait()

    to_log2 = scale * LOG2E
    sink_log2 = sink[number] * LOG2E

    def folded(x, op):
        return functools.reduce(op, [x[r : r + 8] for r in range(0, x.shape[0], 8)])

    def one_block(b, carry):
        rows = pl.ds(pl.multiple_of(b * BLK, BLK), BLK)
        home = b // own_blocks * own_blocks + halo
        query = qd[rows, :HD]
        grad = qd[rows, HD:]
        diag[:BLK, :HD] = query
        diag[BLK:, HD:] = grad
        diag_back[:BLK, :HD] = grad
        diag_back[BLK:, HD:] = query

        def with_slots(live):
            at = [lists[b, j] + home for j in range(live)]
            key_rows = [pl.ds(pl.multiple_of(c * BLK, BLK), BLK) for c in at]
            weights = diag[...]
            top = None
            for j in range(live):
                both = lax.dot_general(kv[key_rows[j], :], weights, NT, preferred_element_type=jnp.float32)
                scored[j] = both
                part = folded(both[:, :BLK], jnp.maximum)
                top = part if top is None else jnp.maximum(top, part)
            top = jnp.maximum(jnp.max(top, axis=0, keepdims=True) * to_log2, sink_log2)
            total = jnp.zeros((8, BLK), jnp.float32)
            dotted = jnp.zeros((8, BLK), jnp.float32)
            for j in range(live):
                power = jnp.exp2(scored[j, :, :BLK] * to_log2 - top)
                scored[j, :, :BLK] = power
                total = total + folded(power, jnp.add)
                dotted = dotted + folded(power * scored[j, :, BLK:], jnp.add)
            sink_power = jnp.exp2(sink_log2 - top)
            inverse = 1.0 / (jnp.sum(total, axis=0, keepdims=True) + sink_power)
            delta = jnp.sum(dotted, axis=0, keepdims=True) * inverse
            sink_acc[...] += sink_power * inverse * delta
            weights = diag_back[...]
            for j in range(live):
                probs = scored[j, :, :BLK] * inverse
                dscores = probs * (scored[j, :, BLK:] - delta)
                pair = jnp.concatenate([probs, dscores], axis=1).astype(jnp.bfloat16)
                paired[pl.ds(j * BLK, BLK), :] = pair
                acc[key_rows[j], :] += lax.dot_general(
                    pair, weights, NN, preferred_element_type=jnp.float32
                )
            attended = lax.dot_general(
                jnp.concatenate([vt[c] for c in at], axis=1),
                paired[: live * BLK, :BLK],
                NN,
                preferred_element_type=jnp.float32,
            )
            query_grad = lax.dot_general(
                jnp.concatenate([kt[c] for c in at], axis=1),
                paired[: live * BLK, BLK:],
                NN,
                preferred_element_type=jnp.float32,
            )
            out[2, rows, :] = attended.astype(jnp.bfloat16).T
            out[3, rows, :] = (query_grad * scale).astype(jnp.bfloat16).T

        for live in range(1, slots + 1):
            pl.when(lists[b, slots] == live)(functools.partial(with_slots, live))
        return carry

    lax.fori_loop(0, blocks, one_block, 0)

    def finish(b, carry):
        rows = pl.ds(pl.multiple_of(b * BLK, BLK), BLK)
        from_rows = pl.ds(pl.multiple_of((b + halo) * BLK, BLK), BLK)
        out[0, rows, :] = acc[from_rows, :HD].astype(jnp.bfloat16)
        out[1, rows, :] = (acc[from_rows, HD:] * scale).astype(jnp.bfloat16)
        return carry

    lax.fori_loop(0, blocks, finish, 0)
    lanes = lax.broadcasted_iota(jnp.int32, (1, BLK), 1)
    sink_sum = jnp.sum(sink_acc[...], axis=1, keepdims=True)
    sink_out[...] = sink_in[...] - jnp.where(lanes == number, sink_sum, 0.0)
    copies = []
    for k in range(group):
        row = pl.multiple_of((spot ^ k) * span, span)
        n, part = leaving["sent"][k]
        to_row = part * 4 * span
        for a in range(4):
            copies.append(
                pltpu.make_async_copy(
                    out.at[a, pl.ds(row, span)],
                    results[n].at[pl.ds(to_row + a * span, span)],
                    out_sems.at[k, a],
                )
            )
    for copy in copies:
        copy.start()
    if halo:
        for side, row in ((0, 0), (1, edge + blocks * BLK)):
            halo_out[side, :, :HD] = acc[pl.ds(row, edge), :HD]
            halo_out[side, :, HD:] = acc[pl.ds(row, edge), HD:] * scale
    for copy in copies:
        copy.wait()


def attend(sink, sink_in, marks_in, parcels, halo_in, routes, group, per_device, head, halo, slots, own_blocks, scale):
    span = own_blocks * BLK
    edge = halo * BLK
    blocks = own_blocks * group
    window = blocks + 2 * halo
    out_shape = [
        jax.ShapeDtypeStruct((n * 4 * span, HD), jnp.bfloat16) for n in routes[1]["rows"]
    ]
    out_specs = [ANY] * len(out_shape) + [VMEM] * 2
    out_shape.append(jax.ShapeDtypeStruct((1, BLK), jnp.float32))
    out_shape.append(jax.ShapeDtypeStruct((blocks, HD), jnp.int32))
    extra = []
    if halo:
        extra = [halo_in]
        out_shape.append(jax.ShapeDtypeStruct((2, edge, 2 * HD), jnp.float32))
        out_specs.append(VMEM)
    return pl.pallas_call(
        functools.partial(
            attend_kernel, group, per_device, head, halo, slots, own_blocks, scale, routes
        ),
        out_shape=out_shape,
        in_specs=[SMEM, VMEM, VMEM] + [ANY] * (len(parcels) + len(extra)),
        out_specs=out_specs,
        scratch_shapes=[
            pltpu.VMEM((window * BLK, 2 * HD), jnp.bfloat16),
            pltpu.VMEM((blocks * BLK, 2 * HD), jnp.bfloat16),
            pltpu.VMEM((group, NOTE, HD), jnp.bfloat16),
            pltpu.SMEM((blocks, HD), jnp.int32),
            pltpu.VMEM((window, HD, BLK), jnp.bfloat16),
            pltpu.VMEM((window, HD, BLK), jnp.bfloat16),
            pltpu.VMEM((2 * BLK, 2 * HD), jnp.bfloat16),
            pltpu.VMEM((2 * BLK, 2 * HD), jnp.bfloat16),
            pltpu.VMEM((slots, BLK, 2 * BLK), jnp.float32),
            pltpu.VMEM((slots * BLK, 2 * BLK), jnp.bfloat16),
            pltpu.VMEM((window * BLK, 2 * HD), jnp.float32),
            pltpu.VMEM((4, blocks * BLK, HD), jnp.bfloat16),
            pltpu.VMEM((1, BLK), jnp.float32),
            pltpu.SemaphoreType.DMA((group + 1, 5)),
            pltpu.SemaphoreType.DMA,
            pltpu.SemaphoreType.DMA((group, 4)),
        ],
        compiler_params=PARAMS,
        cost_estimate=pl.CostEstimate(
            flops=blocks * slots * 64 * BLK * BLK * HD,
            bytes_accessed=blocks * BLK * HD * 16,
            transcendentals=blocks * slots * BLK * BLK,
        ),
        name="attend",
    )(sink, sink_in, marks_in, *parcels, *extra)


def local(queries, keys, values, out_grad, adjacency, counts, sink):
    seq = lax.axis_size("seq")
    group = min(seq, GROUP)
    groups = seq // group
    heads = sink.shape[0]
    per_device = heads // group
    slots = adjacency.shape[2]
    own_blocks = adjacency.shape[1]
    span = own_blocks * BLK
    size = 4 * span
    halo = RADIUS * own_blocks if groups > 1 else 0
    scale = HD ** (-0.5)
    spot = lax.rem(lax.axis_index("seq"), group)

    def swap(x, k, axis="seq"):
        return lax.ppermute(x, axis, [(i, i ^ k) for i in range(lax.axis_size(axis))])

    def between(buffers, route):
        pairs = zip(buffers[1:], route["steps"][1:])
        return [buffers[0]] + [swap(x, k) for x, k in pairs]

    def beside(x, step):
        route = [(i, i + step * group) for i in range(seq) if 0 <= i + step * group < seq]
        return lax.ppermute(x, "seq", route)

    def halos(parcels, route):
        stacked = jnp.stack(
            [parcels[n][row * size : (row + 1) * size] for n, row in route["arrived"]]
        )
        ends = []
        for side, step in ((group - RADIUS, 1), (0, -1)):
            near = [stacked[(side + r) ^ spot] for r in range(RADIUS)]
            near = [jnp.concatenate([x[:span], x[span : 2 * span]], axis=1) for x in near]
            ends.append(beside(jnp.concatenate(near, axis=0), step))
        return jnp.stack(ends)

    def add_halos(results, halo_grads, route):
        stacked = jnp.stack(
            [results[n][row * size : (row + 1) * size] for n, row in route["sent"]]
        )
        for side, step, half in ((group - RADIUS, -1, 0), (0, 1, 1)):
            grads = beside(halo_grads[half], step)
            for r in range(RADIUS):
                at = (side + r) ^ spot
                rows = stacked[at]
                more = grads[r * span : (r + 1) * span]
                more = jnp.concatenate([more[:, :HD], more[:, HD:]], axis=0)
                wide = rows[: 2 * span].astype(jnp.float32) + more
                rows = jnp.concatenate([wide.astype(jnp.bfloat16), rows[2 * span :]], axis=0)
                stacked = lax.dynamic_update_index_in_dim(stacked, rows, at, 0)
        results = list(results)
        for k, (n, row) in enumerate(route["sent"]):
            results[n] = results[n].at[row * size : (row + 1) * size].set(stacked[k])
        return results

    constrained = [
        pltpu.with_memory_space_constraint(x, pltpu.HBM)
        for x in (adjacency, counts, keys, values, queries, out_grad)
    ]
    adjacency, counts, *sources = constrained
    routes_out = [DIRECT] * (per_device - 1) + [PAIRED]

    arrived = []
    packed = []
    for head in range(per_device):
        packed = pack(
            adjacency, counts, sources, packed[:1], DIRECT, group, per_device, head
        )
        crossed = swap(packed[-1], 1)
        buffers = merge(crossed, packed[:-1], DIRECT, size)
        if head > 0:
            buffers[1:] = after(arrived[-1][1:-1], buffers[1:])
        arrived.append(between(buffers, DIRECT) + [crossed])

    sink_row = jnp.zeros((1, BLK), jnp.float32)
    marks = jnp.zeros((own_blocks * group, HD), jnp.int32)
    returned = []
    for head in range(per_device):
        routes = (DIRECT, routes_out[head])
        halo_in = halos(arrived[head], DIRECT) if halo else None
        done = attend(
            sink,
            sink_row,
            marks,
            arrived[head],
            halo_in,
            routes,
            group,
            per_device,
            head,
            halo,
            slots,
            own_blocks,
            scale,
        )
        count = len(routes[1]["rows"])
        results, sink_row, marks = list(done[:count]), done[count], done[count + 1]
        if halo:
            results = add_halos(results, done[count + 2], routes[1])
        if head < per_device - 1:
            results[1:] = after(arrived[head + 1][1:-1], results[1:])
        elif head > 0:
            *results[1:], sink_row = after(returned[-1][1:-1], results[1:] + [sink_row])
        crossed = swap(results[-1], 1)
        buffers = merge(crossed, results[:-1], routes[1], size)
        returned.append(between(buffers, routes[1]) + [crossed])
    outs = []
    for head in range(per_device):
        outs = unpack(returned[head], outs, routes_out[head], group, per_device, head)
    value_grad, key_grad, attended, query_grad = outs
    for axis in ("dp", "seq"):
        step = 1
        while step < lax.axis_size(axis):
            sink_row = sink_row + swap(sink_row, step, axis)
            step *= 2
    return attended, query_grad, key_grad, value_grad, sink_row[0, :heads]


def solution(mesh):
    tokens = P("dp", "seq", None)
    return jax.shard_map(
        local,
        mesh=mesh,
        in_specs=(tokens, tokens, tokens, tokens, tokens, P("dp", "seq"), P()),
        out_specs=(tokens, tokens, tokens, tokens, P()),
        check_vma=False,
    )
```

```python
import functools

import jax
import jax.numpy as jnp
from jax import lax
from jax.experimental import pallas as pl
from jax.experimental.pallas import tpu as pltpu
from jax.sharding import PartitionSpec as P

HD = 128
BLK = 128
RADIUS = 2
GROUP = 8
NOTE = 16
LOG2E = 1.4426950408889634
VMEM_LIMIT = 48 * 1024 * 1024
NT = (((1,), (1,)), ((), ()))
NN = (((1,), (0,)), ((), ()))
ANY = pl.BlockSpec(memory_space=pl.ANY)
SMEM = pl.BlockSpec(memory_space=pltpu.SMEM)
VMEM = pl.BlockSpec(memory_space=pltpu.VMEM)
PARAMS = pltpu.CompilerParams(vmem_limit_bytes=VMEM_LIMIT)


ORDER = (1, 2, 3)
STEPS = (0,) + tuple(2 * m for m in ORDER)
PLACE = {m: n for n, m in enumerate((0,) + ORDER)}
HALVES = tuple((PLACE[k // 2], k % 2) for k in range(GROUP))
SWAP_BEFORE = {
    "steps": STEPS + (1,),
    "sizes": (1, 2, 2, 2, 4),
    "sent": tuple((4, n) if e else (n, 0) for n, e in HALVES),
    "arrived_sizes": (1, 2, 2, 2, 4),
    "arrived": tuple((4, 0) if (n, e) == (0, 1) else (n, e) for n, e in HALVES),
}
SWAP_AFTER = {
    "steps": STEPS,
    "sizes": (2, 2, 2, 2),
    "sent": HALVES,
    "arrived_sizes": (2, 2, 2, 2, 4),
    "arrived": tuple((4, n) if e else (n, 0) for n, e in HALVES),
}


def bytes_cost(count):
    return pl.CostEstimate(flops=0, bytes_accessed=count, transcendentals=0)


def run_copies(copies):
    for copy in copies:
        copy.start()
    for copy in copies:
        copy.wait()


def pack_kernel(group, per_device, tokens, items, noted, awaited, *refs):
    adjacency, counts = refs[:2]
    sources, outs = refs[2:6], refs[6 + awaited : -5]
    slots_here, counts_here, note, sems, list_sems = refs[-5:]
    rank = lax.axis_index("seq")
    spot = lax.rem(rank, group)
    copies = []
    for i, (head, k, n, row) in enumerate(items):
        column = pl.multiple_of(((spot ^ k) * per_device + head) * HD, HD)
        for a, source in enumerate(sources):
            copies.append(
                pltpu.make_async_copy(
                    source.at[0, :, pl.ds(column, HD)],
                    outs[n].at[pl.ds(row + a * tokens, tokens)],
                    sems.at[i, a],
                )
            )
    for copy in copies:
        copy.start()
    if noted:
        run_copies(
            (
                pltpu.make_async_copy(adjacency, slots_here, list_sems.at[0]),
                pltpu.make_async_copy(counts, counts_here, list_sems.at[1]),
            )
        )
        own_blocks, slots = adjacency.shape[1:]
        rows = lax.broadcasted_iota(jnp.int32, note.shape, 0)
        lanes = lax.broadcasted_iota(jnp.int32, note.shape, 1)
        marks = jnp.zeros(note.shape, jnp.int32)
        for b in range(own_blocks):
            for j in range(slots):
                near = slots_here[0, b, j] - rank * own_blocks
                marks = jnp.where((rows == b) & (lanes == j), near, marks)
            marks = jnp.where((rows == b) & (lanes == slots), counts_here[0, b], marks)
        note[...] = marks.astype(jnp.float32)
        for out in outs[:noted]:
            row = out.shape[0] // (4 * tokens) * 4 * tokens
            out[row : row + NOTE, :] = note[...].astype(jnp.bfloat16)
    for copy in copies:
        copy.wait()


def pack(adjacency, counts, sources, awaited, items, parts, noted, group, per_device):
    tokens = sources[0].shape[1]
    size = 4 * tokens
    items = [(head, k, n, part * size) for head, k, n, part in items]
    rows = [n * size + (NOTE if i < noted else 0) for i, n in enumerate(parts)]
    return pl.pallas_call(
        functools.partial(
            pack_kernel, group, per_device, tokens, items, noted, len(awaited)
        ),
        out_shape=[jax.ShapeDtypeStruct((r, HD), jnp.bfloat16) for r in rows],
        in_specs=[ANY] * (6 + len(awaited)),
        out_specs=[VMEM] * len(rows),
        scratch_shapes=[
            pltpu.SMEM(adjacency.shape, jnp.int32),
            pltpu.SMEM(counts.shape, jnp.int32),
            pltpu.VMEM((NOTE, HD), jnp.float32),
            pltpu.SemaphoreType.DMA((len(items), 4)),
            pltpu.SemaphoreType.DMA((2,)),
        ],
        compiler_params=PARAMS,
        cost_estimate=bytes_cost(len(items) * size * HD * 4),
        name="pack",
    )(adjacency, counts, *sources, *awaited)


def pass_kernel(*refs):
    pass


def after(awaited, arrays):
    return pl.pallas_call(
        pass_kernel,
        out_shape=[jax.ShapeDtypeStruct(x.shape, x.dtype) for x in arrays],
        in_specs=[ANY] * (len(arrays) + len(awaited)),
        out_specs=[ANY] * len(arrays),
        input_output_aliases={n: n for n in range(len(arrays))},
        compiler_params=PARAMS,
        cost_estimate=bytes_cost(0),
        name="after",
    )(*arrays, *awaited)


def split_kernel(pairs, size, noted, *refs):
    parcels, out, sems = refs[:pairs], refs[-2], refs[-1]
    copies = []
    for m in range(pairs):
        moves = [(size, m * size, size)]
        if noted:
            moves.append((2 * size, pairs * size + m * NOTE, NOTE))
        for i, (row, to, count) in enumerate(moves):
            copies.append(
                pltpu.make_async_copy(
                    parcels[m].at[pl.ds(row, count)], out.at[pl.ds(to, count)], sems.at[m, i]
                )
            )
    run_copies(copies)


def split(parcels, awaited, size):
    pairs = len(parcels)
    noted = parcels[0].shape[0] > 2 * size
    rows = pairs * (size + NOTE * noted)
    return pl.pallas_call(
        functools.partial(split_kernel, pairs, size, noted),
        out_shape=jax.ShapeDtypeStruct((rows, HD), jnp.bfloat16),
        in_specs=[ANY] * (pairs + len(awaited)),
        out_specs=VMEM,
        scratch_shapes=[pltpu.SemaphoreType.DMA((pairs, 2))],
        compiler_params=PARAMS,
        cost_estimate=bytes_cost(rows * HD * 4),
        name="split",
    )(*parcels, *awaited)


def merge_kernel(size, *refs):
    swapped, outs, sems = refs[0], refs[-4:-1], refs[-1]
    run_copies(
        [
            pltpu.make_async_copy(
                swapped.at[pl.ds((n + 1) * size, size)], out.at[pl.ds(size, size)], sems.at[n]
            )
            for n, out in enumerate(outs)
        ]
    )


def merge(swapped, halves, size):
    return pl.pallas_call(
        functools.partial(merge_kernel, size),
        out_shape=[jax.ShapeDtypeStruct(x.shape, x.dtype) for x in halves],
        in_specs=[VMEM] + [ANY] * len(halves),
        out_specs=[ANY] * len(halves),
        scratch_shapes=[pltpu.SemaphoreType.DMA((len(halves),))],
        input_output_aliases={1 + n: n for n in range(len(halves))},
        compiler_params=PARAMS,
        cost_estimate=bytes_cost(len(halves) * size * HD * 4),
        name="merge",
    )(swapped, *halves)


def unpack_kernel(group, per_device, head, tokens, count, layout, passed, *refs):
    parcels, outs, sems = refs[:count], refs[-5 - passed : -1 - passed], refs[-1]
    spot = lax.rem(lax.axis_index("seq"), group)
    copies = []
    for k, (n, from_row) in enumerate(layout):
        column = pl.multiple_of(((spot ^ k) * per_device + head) * HD, HD)
        for a, out in enumerate(outs):
            copies.append(
                pltpu.make_async_copy(
                    parcels[n].at[pl.ds(from_row + a * tokens, tokens)],
                    out.at[0, :, pl.ds(column, HD)],
                    sems.at[k, a],
                )
            )
    run_copies(copies)


def unpack(parcels, outs, passed, route, group, per_device, head):
    count = len(parcels)
    tokens = parcels[0].shape[0] // (4 * route["sizes"][0])
    layout = [(n, row * 4 * tokens) for n, row in route["arrived"]]
    shape = jax.ShapeDtypeStruct((1, tokens, group * per_device * HD), jnp.bfloat16)
    return pl.pallas_call(
        functools.partial(
            unpack_kernel, group, per_device, head, tokens, count, layout, len(passed)
        ),
        out_shape=[shape] * 4 + [jax.ShapeDtypeStruct(x.shape, x.dtype) for x in passed],
        in_specs=[VMEM] * count + [ANY] * (len(outs) + len(passed)),
        out_specs=[ANY] * (4 + len(passed)),
        scratch_shapes=[pltpu.SemaphoreType.DMA((group, 4))],
        input_output_aliases={
            count + n: 4 - len(outs) + n for n in range(len(outs) + len(passed))
        },
        compiler_params=PARAMS,
        cost_estimate=bytes_cost(group * tokens * HD * 16),
        name="unpack",
    )(*parcels, *outs, *passed)


def attend_kernel(group, per_device, head, halo, slots, own_blocks, scale, route, *refs):
    sink, sink_in, marks_in = refs[:3]
    arriving, leaving = route
    count = len(arriving["arrived_sizes"])
    parcels, refs = refs[3 : 3 + count], refs[3 + count :]
    if halo:
        halo_in, refs = refs[0], refs[1:]
    count = len(leaving["sizes"])
    results, sink_out, marks = refs[:count], refs[count], refs[count + 1]
    refs = refs[count + 2 :]
    if halo:
        halo_out, refs = refs[0], refs[1:]
    kv, qd, notes, lists, kt, vt, diag, diag_back, scored, paired, acc, out = refs[:12]
    sink_acc, sems, list_sem, out_sems = refs[12:]

    blocks = own_blocks * group
    span = own_blocks * BLK
    edge = halo * BLK
    window = blocks + 2 * halo
    spot = lax.rem(lax.axis_index("seq"), group)
    number = spot * per_device + head
    note_copies, copies = [], []
    for k, (n, row) in enumerate(arriving["arrived"] if head == 0 else ()):
        row = arriving["arrived_sizes"][n] * 4 * span + row * NOTE
        note_copies.append(
            pltpu.make_async_copy(
                parcels[n].at[pl.ds(row, NOTE)], notes.at[spot ^ k], sems.at[k, 4]
            )
        )
    for k in range(group):
        row = pl.multiple_of((spot ^ k) * span, span)
        targets = (
            kv.at[pl.ds(row + edge, span), pl.ds(0, HD)],
            kv.at[pl.ds(row + edge, span), pl.ds(HD, HD)],
            qd.at[pl.ds(row, span), pl.ds(0, HD)],
            qd.at[pl.ds(row, span), pl.ds(HD, HD)],
        )
        n, part = arriving["arrived"][k]
        from_row = part * 4 * span
        for a, target in enumerate(targets):
            copies.append(
                pltpu.make_async_copy(
                    parcels[n].at[pl.ds(from_row + a * span, span)], target, sems.at[k, a]
                )
            )
    if halo:
        copies.append(pltpu.make_async_copy(halo_in.at[0], kv.at[pl.ds(0, edge)], sems.at[group, 0]))
        copies.append(
            pltpu.make_async_copy(
                halo_in.at[1], kv.at[pl.ds(edge + blocks * BLK, edge)], sems.at[group, 1]
            )
        )
    for copy in note_copies + copies:
        copy.start()
    diag[...] = jnp.zeros_like(diag)
    diag_back[...] = jnp.zeros_like(diag_back)
    acc[...] = jnp.zeros_like(acc)
    sink_acc[...] = jnp.zeros_like(sink_acc)
    for copy in note_copies:
        copy.wait()
    if head == 0:
        for j in range(group):
            marks[pl.ds(j * own_blocks, own_blocks), :] = (
                notes[j].astype(jnp.float32).astype(jnp.int32)[:own_blocks]
            )
    else:
        marks[...] = marks_in[...]
    list_copy = pltpu.make_async_copy(marks, lists, list_sem)
    list_copy.start()
    for copy in copies:
        copy.wait()

    def turn(c, carry):
        rows = kv[pl.ds(pl.multiple_of(c * BLK, BLK), BLK), :]
        kt[c] = rows[:, :HD].T
        vt[c] = rows[:, HD:].T
        return carry

    lax.fori_loop(0, window, turn, 0)
    list_copy.wait()

    to_log2 = scale * LOG2E
    sink_log2 = sink[number] * LOG2E

    def folded(x, op):
        return functools.reduce(op, [x[r : r + 8] for r in range(0, x.shape[0], 8)])

    def one_block(b, carry):
        rows = pl.ds(pl.multiple_of(b * BLK, BLK), BLK)
        home = b // own_blocks * own_blocks + halo
        query = qd[rows, :HD]
        grad = qd[rows, HD:]
        diag[:BLK, :HD] = query
        diag[BLK:, HD:] = grad
        diag_back[:BLK, :HD] = grad
        diag_back[BLK:, HD:] = query

        def with_slots(live):
            at = [lists[b, j] + home for j in range(live)]
            key_rows = [pl.ds(pl.multiple_of(c * BLK, BLK), BLK) for c in at]
            weights = diag[...]
            top = None
            for j in range(live):
                both = lax.dot_general(kv[key_rows[j], :], weights, NT, preferred_element_type=jnp.float32)
                scored[j] = both
                part = folded(both[:, :BLK], jnp.maximum)
                top = part if top is None else jnp.maximum(top, part)
            top = jnp.maximum(jnp.max(top, axis=0, keepdims=True) * to_log2, sink_log2)
            total = jnp.zeros((8, BLK), jnp.float32)
            dotted = jnp.zeros((8, BLK), jnp.float32)
            for j in range(live):
                power = jnp.exp2(scored[j, :, :BLK] * to_log2 - top)
                scored[j, :, :BLK] = power
                total = total + folded(power, jnp.add)
                dotted = dotted + folded(power * scored[j, :, BLK:], jnp.add)
            sink_power = jnp.exp2(sink_log2 - top)
            inverse = 1.0 / (jnp.sum(total, axis=0, keepdims=True) + sink_power)
            delta = jnp.sum(dotted, axis=0, keepdims=True) * inverse
            sink_acc[...] += sink_power * inverse * delta
            weights = diag_back[...]
            for j in range(live):
                probs = scored[j, :, :BLK] * inverse
                dscores = probs * (scored[j, :, BLK:] - delta)
                pair = jnp.concatenate([probs, dscores], axis=1).astype(jnp.bfloat16)
                paired[pl.ds(j * BLK, BLK), :] = pair
                acc[key_rows[j], :] += lax.dot_general(
                    pair, weights, NN, preferred_element_type=jnp.float32
                )
            attended = lax.dot_general(
                jnp.concatenate([vt[c] for c in at], axis=1),
                paired[: live * BLK, :BLK],
                NN,
                preferred_element_type=jnp.float32,
            )
            query_grad = lax.dot_general(
                jnp.concatenate([kt[c] for c in at], axis=1),
                paired[: live * BLK, BLK:],
                NN,
                preferred_element_type=jnp.float32,
            )
            out[2, rows, :] = attended.astype(jnp.bfloat16).T
            out[3, rows, :] = (query_grad * scale).astype(jnp.bfloat16).T

        for live in range(1, slots + 1):
            pl.when(lists[b, slots] == live)(functools.partial(with_slots, live))
        return carry

    lax.fori_loop(0, blocks, one_block, 0)

    def finish(b, carry):
        rows = pl.ds(pl.multiple_of(b * BLK, BLK), BLK)
        from_rows = pl.ds(pl.multiple_of((b + halo) * BLK, BLK), BLK)
        out[0, rows, :] = acc[from_rows, :HD].astype(jnp.bfloat16)
        out[1, rows, :] = (acc[from_rows, HD:] * scale).astype(jnp.bfloat16)
        return carry

    lax.fori_loop(0, blocks, finish, 0)
    lanes = lax.broadcasted_iota(jnp.int32, (1, BLK), 1)
    sink_sum = jnp.sum(sink_acc[...], axis=1, keepdims=True)
    sink_out[...] = sink_in[...] - jnp.where(lanes == number, sink_sum, 0.0)
    copies = []
    for k in range(group):
        row = pl.multiple_of((spot ^ k) * span, span)
        n, part = leaving["sent"][k]
        to_row = part * 4 * span
        for a in range(4):
            copies.append(
                pltpu.make_async_copy(
                    out.at[a, pl.ds(row, span)],
                    results[n].at[pl.ds(to_row + a * span, span)],
                    out_sems.at[k, a],
                )
            )
    for copy in copies:
        copy.start()
    if halo:
        for side, row in ((0, 0), (1, edge + blocks * BLK)):
            halo_out[side, :, :HD] = acc[pl.ds(row, edge), :HD]
            halo_out[side, :, HD:] = acc[pl.ds(row, edge), HD:] * scale
    for copy in copies:
        copy.wait()


def attend(sink, sink_in, marks_in, parcels, halo_in, routes, group, per_device, head, halo, slots, own_blocks, scale):
    span = own_blocks * BLK
    edge = halo * BLK
    blocks = own_blocks * group
    window = blocks + 2 * halo
    out_shape = [
        jax.ShapeDtypeStruct((n * 4 * span, HD), jnp.bfloat16) for n in routes[1]["sizes"]
    ]
    out_specs = [ANY] * len(out_shape) + [VMEM] * 2
    out_shape.append(jax.ShapeDtypeStruct((1, BLK), jnp.float32))
    out_shape.append(jax.ShapeDtypeStruct((blocks, HD), jnp.int32))
    extra = []
    if halo:
        extra = [halo_in]
        out_shape.append(jax.ShapeDtypeStruct((2, edge, 2 * HD), jnp.float32))
        out_specs.append(VMEM)
    return pl.pallas_call(
        functools.partial(
            attend_kernel, group, per_device, head, halo, slots, own_blocks, scale, routes
        ),
        out_shape=out_shape,
        in_specs=[SMEM, VMEM, VMEM] + [ANY] * (len(parcels) + len(extra)),
        out_specs=out_specs,
        scratch_shapes=[
            pltpu.VMEM((window * BLK, 2 * HD), jnp.bfloat16),
            pltpu.VMEM((blocks * BLK, 2 * HD), jnp.bfloat16),
            pltpu.VMEM((group, NOTE, HD), jnp.bfloat16),
            pltpu.SMEM((blocks, HD), jnp.int32),
            pltpu.VMEM((window, HD, BLK), jnp.bfloat16),
            pltpu.VMEM((window, HD, BLK), jnp.bfloat16),
            pltpu.VMEM((2 * BLK, 2 * HD), jnp.bfloat16),
            pltpu.VMEM((2 * BLK, 2 * HD), jnp.bfloat16),
            pltpu.VMEM((slots, BLK, 2 * BLK), jnp.float32),
            pltpu.VMEM((slots * BLK, 2 * BLK), jnp.bfloat16),
            pltpu.VMEM((window * BLK, 2 * HD), jnp.float32),
            pltpu.VMEM((4, blocks * BLK, HD), jnp.bfloat16),
            pltpu.VMEM((1, BLK), jnp.float32),
            pltpu.SemaphoreType.DMA((group + 1, 5)),
            pltpu.SemaphoreType.DMA,
            pltpu.SemaphoreType.DMA((group, 4)),
        ],
        compiler_params=PARAMS,
        cost_estimate=pl.CostEstimate(
            flops=blocks * slots * 64 * BLK * BLK * HD,
            bytes_accessed=blocks * BLK * HD * 16,
            transcendentals=blocks * slots * BLK * BLK,
        ),
        name="attend",
    )(sink, sink_in, marks_in, *parcels, *extra)


def local(queries, keys, values, out_grad, adjacency, counts, sink):
    seq = lax.axis_size("seq")
    group = min(seq, GROUP)
    groups = seq // group
    heads = sink.shape[0]
    per_device = heads // group
    slots = adjacency.shape[2]
    own_blocks = adjacency.shape[1]
    span = own_blocks * BLK
    size = 4 * span
    halo = RADIUS * own_blocks if groups > 1 else 0
    scale = HD ** (-0.5)
    spot = lax.rem(lax.axis_index("seq"), group)

    def swap(x, k, axis="seq"):
        return lax.ppermute(x, axis, [(i, i ^ k) for i in range(lax.axis_size(axis))])

    def beside(x, step):
        route = [(i, i + step * group) for i in range(seq) if 0 <= i + step * group < seq]
        return lax.ppermute(x, "seq", route)

    def halos(parcels, route):
        stacked = jnp.stack(
            [parcels[n][row * size : (row + 1) * size] for n, row in route["arrived"]]
        )
        ends = []
        for side, step in ((group - RADIUS, 1), (0, -1)):
            near = [stacked[(side + r) ^ spot] for r in range(RADIUS)]
            near = [jnp.concatenate([x[:span], x[span : 2 * span]], axis=1) for x in near]
            ends.append(beside(jnp.concatenate(near, axis=0), step))
        return jnp.stack(ends)

    def add_halos(results, halo_grads, route):
        stacked = jnp.stack(
            [results[n][row * size : (row + 1) * size] for n, row in route["sent"]]
        )
        for side, step, half in ((group - RADIUS, -1, 0), (0, 1, 1)):
            grads = beside(halo_grads[half], step)
            for r in range(RADIUS):
                at = (side + r) ^ spot
                rows = stacked[at]
                more = grads[r * span : (r + 1) * span]
                more = jnp.concatenate([more[:, :HD], more[:, HD:]], axis=0)
                wide = rows[: 2 * span].astype(jnp.float32) + more
                rows = jnp.concatenate([wide.astype(jnp.bfloat16), rows[2 * span :]], axis=0)
                stacked = lax.dynamic_update_index_in_dim(stacked, rows, at, 0)
        results = list(results)
        for k, (n, row) in enumerate(route["sent"]):
            results[n] = results[n].at[row * size : (row + 1) * size].set(stacked[k])
        return results

    constrained = [
        pltpu.with_memory_space_constraint(x, pltpu.HBM)
        for x in (adjacency, counts, keys, values, queries, out_grad)
    ]
    adjacency, counts, *sources = constrained
    shared = (adjacency, counts, sources)
    items = [(0, k, n, part) for k, (n, part) in enumerate(SWAP_AFTER["sent"])]
    sizes = list(SWAP_AFTER["sizes"])
    noted = len(sizes)
    cross = len(SWAP_BEFORE["sizes"]) - 1
    sent = list(enumerate(SWAP_BEFORE["sent"]))
    for head in range(1, per_device):
        items += [(head, k, len(sizes), part) for k, (n, part) in sent if n == cross]
        sizes.append(SWAP_BEFORE["sizes"][cross])
    packed = pack(*shared, [], items, sizes, noted, group, per_device)
    filled = []
    for head in range(1, per_device):
        items = [(head, k, n, part) for k, (n, part) in sent if n != cross]
        own, *halves = pack(
            *shared, packed[:1], items, SWAP_BEFORE["sizes"][:cross], 0, group, per_device
        )
        crossed = swap(packed[noted + head - 1], 1)
        filled.append((own, merge(crossed, halves, size), crossed))
    between = SWAP_AFTER["steps"][1:]
    parcels = [packed[0]] + [swap(x, k) for x, k in zip(packed[1:noted], between)]
    awaited = [halves[0] for _, halves, _ in filled]
    arrived = [parcels + [swap(split(parcels, awaited, size), 1)]]
    routes_in = [SWAP_AFTER] + [SWAP_BEFORE] * (per_device - 1)
    for own, halves, crossed in filled:
        halves = after(arrived[-1][1:-1], halves)
        arrived.append([own] + [swap(x, k) for x, k in zip(halves, between)] + [crossed])

    routes_out = [SWAP_AFTER] * (per_device - 1) + [SWAP_BEFORE]
    sink_row = jnp.zeros((1, BLK), jnp.float32)
    marks = jnp.zeros((own_blocks * group, HD), jnp.int32)
    before = arrived[-1][1:-1] if per_device > 1 else []
    returned = []
    for head in range(per_device):
        routes = (routes_in[head], routes_out[head])
        halo_in = halos(arrived[head], routes[0]) if halo else None
        done = attend(
            sink,
            sink_row,
            marks,
            arrived[head],
            halo_in,
            routes,
            group,
            per_device,
            head,
            halo,
            slots,
            own_blocks,
            scale,
        )
        count = len(routes[1]["sizes"])
        results, sink_row, marks = list(done[:count]), done[count], done[count + 1]
        if halo:
            results = add_halos(results, done[count + 2], routes[1])
        if before:
            results[1:] = after(before, results[1:])
        own, *halves = results
        if routes[1] is SWAP_BEFORE:
            crossed = swap(halves.pop(), 1)
            halves = merge(crossed, halves, size)
        before = [swap(x, k) for x, k in zip(halves, between)]
        returned.append([own] + before)
    returned[-1].append(crossed)
    for axis, step in (("dp", 1), ("seq", group)):
        while step < lax.axis_size(axis):
            sink_row = sink_row + swap(sink_row, step, axis)
            step *= 2
    sink_row = sink_row + swap(sink_row, 1)
    outs = []
    for head in range(per_device - 1):
        parcels = returned[head] + [swap(split(returned[head], [crossed], size), 1)]
        *outs, sink_row = unpack(
            parcels, outs, [sink_row], routes_out[head], group, per_device, head
        )
    sink_row = functools.reduce(jnp.add, [sink_row] + [swap(sink_row, k) for k in between])
    outs = unpack(returned[-1], outs, [], routes_out[-1], group, per_device, per_device - 1)
    value_grad, key_grad, attended, query_grad = outs
    return attended, query_grad, key_grad, value_grad, sink_row[0, :heads]


def solution(mesh):
    tokens = P("dp", "seq", None)
    return jax.shard_map(
        local,
        mesh=mesh,
        in_specs=(tokens, tokens, tokens, tokens, tokens, P("dp", "seq"), P()),
        out_specs=(tokens, tokens, tokens, tokens, P()),
        check_vma=False,
    )
```

```python
import functools

import jax
import jax.numpy as jnp
from jax import lax
from jax.experimental import pallas as pl
from jax.experimental.pallas import tpu as pltpu
from jax.sharding import PartitionSpec as P

HD = 128
BLK = 128
RADIUS = 2
GROUP = 8
NOTE = 16
WORK = 20_000_000_000
LOG2E = 1.4426950408889634
VMEM_LIMIT = 48 * 1024 * 1024
NT = (((1,), (1,)), ((), ()))
NN = (((1,), (0,)), ((), ()))
ANY = pl.BlockSpec(memory_space=pl.ANY)
SMEM = pl.BlockSpec(memory_space=pltpu.SMEM)
VMEM = pl.BlockSpec(memory_space=pltpu.VMEM)
PARAMS = pltpu.CompilerParams(vmem_limit_bytes=VMEM_LIMIT)


ORDER = (1, 2, 3)
STEPS = (0,) + tuple(2 * m for m in ORDER)
PLACE = {m: n for n, m in enumerate((0,) + ORDER)}
HALVES = tuple((PLACE[k // 2], k % 2) for k in range(GROUP))
SWAP_BEFORE = {
    "steps": STEPS + (1,),
    "sizes": (1, 2, 2, 2, 4),
    "sent": tuple((4, n) if e else (n, 0) for n, e in HALVES),
    "arrived_sizes": (1, 2, 2, 2, 4),
    "arrived": tuple((4, 0) if (n, e) == (0, 1) else (n, e) for n, e in HALVES),
}
SWAP_SOME = {
    "steps": (0, 4, 6, 2, 3, 1),
    "sizes": (1, 2, 2, 1, 1, 3),
    "sent": ((0, 0), (5, 0), (3, 0), (4, 0), (1, 0), (5, 1), (2, 0), (5, 2)),
    "arrived_sizes": (1, 2, 2, 1, 1, 3),
    "arrived": ((0, 0), (5, 0), (3, 0), (4, 0), (1, 0), (1, 1), (2, 0), (2, 1)),
}
SWAP_AFTER = {
    "steps": STEPS,
    "sizes": (2, 2, 2, 2),
    "sent": HALVES,
    "arrived_sizes": (2, 2, 2, 2, 4),
    "arrived": tuple((4, n) if e else (n, 0) for n, e in HALVES),
}
SWAP_TWICE = {
    "steps": STEPS,
    "sizes": (2, 2, 2, 2),
    "sent": HALVES,
    "arrived_sizes": (2, 2, 2, 2, 2, 2),
    "arrived": tuple((4 + n // 2, n % 2) if e else (n, 0) for n, e in HALVES),
}


def bytes_cost(count):
    return pl.CostEstimate(flops=0, bytes_accessed=count, transcendentals=0)


def run_copies(copies):
    for copy in copies:
        copy.start()
    for copy in copies:
        copy.wait()


def pack_kernel(group, per_device, tokens, items, noted, awaited, *refs):
    adjacency, counts = refs[:2]
    sources, outs = refs[2:6], refs[6 + awaited : -5]
    slots_here, counts_here, note, sems, list_sems = refs[-5:]
    rank = lax.axis_index("seq")
    spot = lax.rem(rank, group)
    copies = []
    for i, (head, k, n, row) in enumerate(items):
        column = pl.multiple_of(((spot ^ k) * per_device + head) * HD, HD)
        for a, source in enumerate(sources):
            copies.append(
                pltpu.make_async_copy(
                    source.at[0, :, pl.ds(column, HD)],
                    outs[n].at[pl.ds(row + a * tokens, tokens)],
                    sems.at[i, a],
                )
            )
    for copy in copies:
        copy.start()
    if noted:
        run_copies(
            (
                pltpu.make_async_copy(adjacency, slots_here, list_sems.at[0]),
                pltpu.make_async_copy(counts, counts_here, list_sems.at[1]),
            )
        )
        own_blocks, slots = adjacency.shape[1:]
        rows = lax.broadcasted_iota(jnp.int32, note.shape, 0)
        lanes = lax.broadcasted_iota(jnp.int32, note.shape, 1)
        marks = jnp.zeros(note.shape, jnp.int32)
        for b in range(own_blocks):
            for j in range(slots):
                near = slots_here[0, b, j] - rank * own_blocks
                marks = jnp.where((rows == b) & (lanes == j), near, marks)
            marks = jnp.where((rows == b) & (lanes == slots), counts_here[0, b], marks)
        note[...] = marks.astype(jnp.float32)
        for out in outs[:noted]:
            row = out.shape[0] // (4 * tokens) * 4 * tokens
            out[row : row + NOTE, :] = note[...].astype(jnp.bfloat16)
    for copy in copies:
        copy.wait()


def pack(adjacency, counts, sources, awaited, items, parts, noted, group, per_device):
    tokens = sources[0].shape[1]
    size = 4 * tokens
    items = [(head, k, n, part * size) for head, k, n, part in items]
    rows = [n * size + (NOTE if i < noted else 0) for i, n in enumerate(parts)]
    return pl.pallas_call(
        functools.partial(
            pack_kernel, group, per_device, tokens, items, noted, len(awaited)
        ),
        out_shape=[jax.ShapeDtypeStruct((r, HD), jnp.bfloat16) for r in rows],
        in_specs=[ANY] * (6 + len(awaited)),
        out_specs=[VMEM] * len(rows),
        scratch_shapes=[
            pltpu.SMEM(adjacency.shape, jnp.int32),
            pltpu.SMEM(counts.shape, jnp.int32),
            pltpu.VMEM((NOTE, HD), jnp.float32),
            pltpu.SemaphoreType.DMA((len(items), 4)),
            pltpu.SemaphoreType.DMA((2,)),
        ],
        compiler_params=PARAMS,
        cost_estimate=bytes_cost(len(items) * size * HD * 4),
        name="pack",
    )(adjacency, counts, *sources, *awaited)


def pass_kernel(*refs):
    pass


def after(awaited, arrays):
    return pl.pallas_call(
        pass_kernel,
        out_shape=[jax.ShapeDtypeStruct(x.shape, x.dtype) for x in arrays],
        in_specs=[ANY] * (len(arrays) + len(awaited)),
        out_specs=[ANY] * len(arrays),
        input_output_aliases={n: n for n in range(len(arrays))},
        compiler_params=PARAMS,
        cost_estimate=bytes_cost(0),
        name="after",
    )(*arrays, *awaited)


def split_kernel(pairs, size, noted, *refs):
    parcels, out, sems = refs[:pairs], refs[-2], refs[-1]
    copies = []
    for m in range(pairs):
        moves = [(size, m * size, size)]
        if noted:
            moves.append((2 * size, pairs * size + m * NOTE, NOTE))
        for i, (row, to, count) in enumerate(moves):
            copies.append(
                pltpu.make_async_copy(
                    parcels[m].at[pl.ds(row, count)], out.at[pl.ds(to, count)], sems.at[m, i]
                )
            )
    run_copies(copies)


def split(parcels, awaited, size, work=0):
    pairs = len(parcels)
    noted = parcels[0].shape[0] > 2 * size
    rows = pairs * (size + NOTE * noted)
    return pl.pallas_call(
        functools.partial(split_kernel, pairs, size, noted),
        out_shape=jax.ShapeDtypeStruct((rows, HD), jnp.bfloat16),
        in_specs=[ANY] * (pairs + len(awaited)),
        out_specs=VMEM,
        scratch_shapes=[pltpu.SemaphoreType.DMA((pairs, 2))],
        compiler_params=PARAMS,
        cost_estimate=pl.CostEstimate(
            flops=work, bytes_accessed=rows * HD * 4, transcendentals=0
        ),
        name="split",
    )(*parcels, *awaited)


def merge_kernel(size, count, noted, *refs):
    swapped, sems = refs[0], refs[-1]
    outs = refs[1 + count + noted : 1 + 2 * count + noted]
    if noted:
        rows = swapped[(count + 1) * size :, :].astype(jnp.float32)
        refs[-2][...] = refs[1][...] + jnp.sum(rows, axis=0, keepdims=True)
    run_copies(
        [
            pltpu.make_async_copy(
                swapped.at[pl.ds((n + 1) * size, size)], out.at[pl.ds(size, size)], sems.at[n]
            )
            for n, out in enumerate(outs)
        ]
    )


def merge(swapped, rows, halves, size):
    held = list(halves) + list(rows)
    return pl.pallas_call(
        functools.partial(merge_kernel, size, len(halves), len(rows)),
        out_shape=[jax.ShapeDtypeStruct(x.shape, x.dtype) for x in held],
        in_specs=[VMEM] * (1 + len(rows)) + [ANY] * len(halves),
        out_specs=[ANY] * len(halves) + [VMEM] * len(rows),
        scratch_shapes=[pltpu.SemaphoreType.DMA((len(halves),))],
        input_output_aliases={1 + len(rows) + n: n for n in range(len(halves))},
        compiler_params=PARAMS,
        cost_estimate=bytes_cost(len(halves) * size * HD * 4),
        name="merge",
    )(swapped, *rows, *halves)


def unpack_kernel(group, per_device, head, tokens, count, layout, passed, rows, *refs):
    parcels, sems = refs[:count], refs[-1]
    tail = passed + (rows > 0)
    outs = refs[-5 - tail : -1 - tail]
    if rows:
        total = functools.reduce(jnp.add, [row[...] for row in refs[count : count + rows]])
        refs[-2][...] = total[0, : group * per_device]
    spot = lax.rem(lax.axis_index("seq"), group)
    copies = []
    for i, (k, n, from_row) in enumerate(layout):
        column = pl.multiple_of(((spot ^ k) * per_device + head) * HD, HD)
        for a, out in enumerate(outs):
            copies.append(
                pltpu.make_async_copy(
                    parcels[n].at[pl.ds(from_row + a * tokens, tokens)],
                    out.at[0, :, pl.ds(column, HD)],
                    sems.at[i, a],
                )
            )
    run_copies(copies)


def unpack(parcels, which, outs, passed, route, tokens, group, per_device, head, work=0, rows=()):
    count = len(which)
    layout = [
        (k, which.index(n), row * 4 * tokens)
        for k, (n, row) in enumerate(route["arrived"])
        if n in which
    ]
    parcels = [parcels[n] for n in which]
    total = [jax.ShapeDtypeStruct((group * per_device,), jnp.float32)] if rows else []
    shape = jax.ShapeDtypeStruct((1, tokens, group * per_device * HD), jnp.bfloat16)
    return pl.pallas_call(
        functools.partial(
            unpack_kernel, group, per_device, head, tokens, count, layout, len(passed), len(rows)
        ),
        out_shape=[shape] * 4 + [jax.ShapeDtypeStruct(x.shape, x.dtype) for x in passed] + total,
        in_specs=[VMEM] * (count + len(rows)) + [ANY] * (len(outs) + len(passed)),
        out_specs=[ANY] * (4 + len(passed)) + [VMEM] * len(total),
        scratch_shapes=[pltpu.SemaphoreType.DMA((len(layout), 4))],
        input_output_aliases={
            count + len(rows) + n: 4 - len(outs) + n for n in range(len(outs) + len(passed))
        },
        compiler_params=PARAMS,
        cost_estimate=pl.CostEstimate(
            flops=work, bytes_accessed=len(layout) * tokens * HD * 16, transcendentals=0
        ),
        name="unpack",
    )(*parcels, *rows, *outs, *passed)


def attend_kernel(group, per_device, head, halo, slots, own_blocks, scale, route, *refs):
    sink, sink_in, marks_in = refs[:3]
    arriving, leaving = route
    count = len(arriving["arrived_sizes"])
    parcels, refs = refs[3 : 3 + count], refs[3 + count :]
    if halo:
        halo_in, refs = refs[0], refs[1:]
    count = len(leaving["sizes"])
    results, sink_out, marks = refs[:count], refs[count], refs[count + 1]
    refs = refs[count + 2 :]
    if halo:
        halo_out, refs = refs[0], refs[1:]
    kv, qd, notes, lists, kt, vt, diag, diag_back, scored, paired, acc, out = refs[:12]
    sink_acc, sink_note, sems, list_sem, out_sems = refs[12:]

    blocks = own_blocks * group
    span = own_blocks * BLK
    edge = halo * BLK
    window = blocks + 2 * halo
    spot = lax.rem(lax.axis_index("seq"), group)
    number = spot * per_device + head
    note_copies, copies = [], []
    for k, (n, row) in enumerate(arriving["arrived"] if head == 0 else ()):
        row = arriving["arrived_sizes"][n] * 4 * span + row * NOTE
        note_copies.append(
            pltpu.make_async_copy(
                parcels[n].at[pl.ds(row, NOTE)], notes.at[spot ^ k], sems.at[k, 4]
            )
        )
    for k in range(group):
        row = pl.multiple_of((spot ^ k) * span, span)
        targets = (
            kv.at[pl.ds(row + edge, span), pl.ds(0, HD)],
            kv.at[pl.ds(row + edge, span), pl.ds(HD, HD)],
            qd.at[pl.ds(row, span), pl.ds(0, HD)],
            qd.at[pl.ds(row, span), pl.ds(HD, HD)],
        )
        n, part = arriving["arrived"][k]
        from_row = part * 4 * span
        for a, target in enumerate(targets):
            copies.append(
                pltpu.make_async_copy(
                    parcels[n].at[pl.ds(from_row + a * span, span)], target, sems.at[k, a]
                )
            )
    if halo:
        copies.append(pltpu.make_async_copy(halo_in.at[0], kv.at[pl.ds(0, edge)], sems.at[group, 0]))
        copies.append(
            pltpu.make_async_copy(
                halo_in.at[1], kv.at[pl.ds(edge + blocks * BLK, edge)], sems.at[group, 1]
            )
        )
    for copy in note_copies + copies:
        copy.start()
    diag[...] = jnp.zeros_like(diag)
    diag_back[...] = jnp.zeros_like(diag_back)
    acc[...] = jnp.zeros_like(acc)
    sink_acc[...] = jnp.zeros_like(sink_acc)
    for copy in note_copies:
        copy.wait()
    if head == 0:
        for j in range(group):
            marks[pl.ds(j * own_blocks, own_blocks), :] = (
                notes[j].astype(jnp.float32).astype(jnp.int32)[:own_blocks]
            )
    else:
        marks[...] = marks_in[...]
    list_copy = pltpu.make_async_copy(marks, lists, list_sem)
    list_copy.start()
    for copy in copies:
        copy.wait()

    def turn(c, carry):
        rows = kv[pl.ds(pl.multiple_of(c * BLK, BLK), BLK), :]
        kt[c] = rows[:, :HD].T
        vt[c] = rows[:, HD:].T
        return carry

    lax.fori_loop(0, window, turn, 0)
    list_copy.wait()

    to_log2 = scale * LOG2E
    sink_log2 = sink[number] * LOG2E

    def folded(x, op):
        return functools.reduce(op, [x[r : r + 8] for r in range(0, x.shape[0], 8)])

    def one_block(b, carry):
        rows = pl.ds(pl.multiple_of(b * BLK, BLK), BLK)
        home = b // own_blocks * own_blocks + halo
        query = qd[rows, :HD]
        grad = qd[rows, HD:]
        diag[:BLK, :HD] = query
        diag[BLK:, HD:] = grad
        diag_back[:BLK, :HD] = grad
        diag_back[BLK:, HD:] = query

        def with_slots(live):
            at = [lists[b, j] + home for j in range(live)]
            key_rows = [pl.ds(pl.multiple_of(c * BLK, BLK), BLK) for c in at]
            weights = diag[...]
            top = None
            for j in range(live):
                both = lax.dot_general(kv[key_rows[j], :], weights, NT, preferred_element_type=jnp.float32)
                scored[j] = both
                part = folded(both[:, :BLK], jnp.maximum)
                top = part if top is None else jnp.maximum(top, part)
            top = jnp.maximum(jnp.max(top, axis=0, keepdims=True) * to_log2, sink_log2)
            total = jnp.zeros((8, BLK), jnp.float32)
            dotted = jnp.zeros((8, BLK), jnp.float32)
            for j in range(live):
                power = jnp.exp2(scored[j, :, :BLK] * to_log2 - top)
                scored[j, :, :BLK] = power
                total = total + folded(power, jnp.add)
                dotted = dotted + folded(power * scored[j, :, BLK:], jnp.add)
            sink_power = jnp.exp2(sink_log2 - top)
            inverse = 1.0 / (jnp.sum(total, axis=0, keepdims=True) + sink_power)
            delta = jnp.sum(dotted, axis=0, keepdims=True) * inverse
            sink_acc[...] += sink_power * inverse * delta
            weights = diag_back[...]
            for j in range(live):
                probs = scored[j, :, :BLK] * inverse
                dscores = probs * (scored[j, :, BLK:] - delta)
                pair = jnp.concatenate([probs, dscores], axis=1).astype(jnp.bfloat16)
                paired[pl.ds(j * BLK, BLK), :] = pair
                acc[key_rows[j], :] += lax.dot_general(
                    pair, weights, NN, preferred_element_type=jnp.float32
                )
            attended = lax.dot_general(
                jnp.concatenate([vt[c] for c in at], axis=1),
                paired[: live * BLK, :BLK],
                NN,
                preferred_element_type=jnp.float32,
            )
            query_grad = lax.dot_general(
                jnp.concatenate([kt[c] for c in at], axis=1),
                paired[: live * BLK, BLK:],
                NN,
                preferred_element_type=jnp.float32,
            )
            out[2, rows, :] = attended.astype(jnp.bfloat16).T
            out[3, rows, :] = (query_grad * scale).astype(jnp.bfloat16).T

        for live in range(1, slots + 1):
            pl.when(lists[b, slots] == live)(functools.partial(with_slots, live))
        return carry

    lax.fori_loop(0, blocks, one_block, 0)

    def finish(b, carry):
        rows = pl.ds(pl.multiple_of(b * BLK, BLK), BLK)
        from_rows = pl.ds(pl.multiple_of((b + halo) * BLK, BLK), BLK)
        out[0, rows, :] = acc[from_rows, :HD].astype(jnp.bfloat16)
        out[1, rows, :] = (acc[from_rows, HD:] * scale).astype(jnp.bfloat16)
        return carry

    lax.fori_loop(0, blocks, finish, 0)
    lanes = lax.broadcasted_iota(jnp.int32, (1, BLK), 1)
    sink_sum = jnp.sum(sink_acc[...], axis=1, keepdims=True)
    sink_row = sink_in[...] - jnp.where(lanes == number, sink_sum, 0.0)
    sink_out[...] = sink_row
    copies = []
    if leaving is SWAP_SOME:
        lines = lax.broadcasted_iota(jnp.int32, (NOTE, BLK), 0)
        rest, rows = sink_row, jnp.zeros((NOTE, BLK), jnp.float32)
        for line in range(3):
            piece = rest.astype(jnp.bfloat16).astype(jnp.float32)
            rows = jnp.where(lines == line, piece, rows)
            rest = rest - piece
        sink_note[...] = rows.astype(jnp.bfloat16)
        room = results[-1].at[pl.ds(leaving["sizes"][-1] * 4 * span, NOTE)]
        copies.append(pltpu.make_async_copy(sink_note, room, out_sems.at[group, 0]))
    for k in range(group):
        row = pl.multiple_of((spot ^ k) * span, span)
        n, part = leaving["sent"][k]
        to_row = part * 4 * span
        for a in range(4):
            copies.append(
                pltpu.make_async_copy(
                    out.at[a, pl.ds(row, span)],
                    results[n].at[pl.ds(to_row + a * span, span)],
                    out_sems.at[k, a],
                )
            )
    for copy in copies:
        copy.start()
    if halo:
        for side, row in ((0, 0), (1, edge + blocks * BLK)):
            halo_out[side, :, :HD] = acc[pl.ds(row, edge), :HD]
            halo_out[side, :, HD:] = acc[pl.ds(row, edge), HD:] * scale
    for copy in copies:
        copy.wait()


def attend(sink, sink_in, marks_in, parcels, halo_in, routes, group, per_device, head, halo, slots, own_blocks, scale):
    span = own_blocks * BLK
    edge = halo * BLK
    blocks = own_blocks * group
    window = blocks + 2 * halo
    rows = [n * 4 * span for n in routes[1]["sizes"]]
    if routes[1] is SWAP_SOME:
        rows[-1] += NOTE
    out_shape = [jax.ShapeDtypeStruct((n, HD), jnp.bfloat16) for n in rows]
    out_specs = [ANY] * len(out_shape) + [VMEM] * 2
    out_shape.append(jax.ShapeDtypeStruct((1, BLK), jnp.float32))
    out_shape.append(jax.ShapeDtypeStruct((blocks, HD), jnp.int32))
    extra = []
    if halo:
        extra = [halo_in]
        out_shape.append(jax.ShapeDtypeStruct((2, edge, 2 * HD), jnp.float32))
        out_specs.append(VMEM)
    return pl.pallas_call(
        functools.partial(
            attend_kernel, group, per_device, head, halo, slots, own_blocks, scale, routes
        ),
        out_shape=out_shape,
        in_specs=[SMEM, VMEM, VMEM] + [ANY] * (len(parcels) + len(extra)),
        out_specs=out_specs,
        scratch_shapes=[
            pltpu.VMEM((window * BLK, 2 * HD), jnp.bfloat16),
            pltpu.VMEM((blocks * BLK, 2 * HD), jnp.bfloat16),
            pltpu.VMEM((group, NOTE, HD), jnp.bfloat16),
            pltpu.SMEM((blocks, HD), jnp.int32),
            pltpu.VMEM((window, HD, BLK), jnp.bfloat16),
            pltpu.VMEM((window, HD, BLK), jnp.bfloat16),
            pltpu.VMEM((2 * BLK, 2 * HD), jnp.bfloat16),
            pltpu.VMEM((2 * BLK, 2 * HD), jnp.bfloat16),
            pltpu.VMEM((slots, BLK, 2 * BLK), jnp.float32),
            pltpu.VMEM((slots * BLK, 2 * BLK), jnp.bfloat16),
            pltpu.VMEM((window * BLK, 2 * HD), jnp.float32),
            pltpu.VMEM((4, blocks * BLK, HD), jnp.bfloat16),
            pltpu.VMEM((1, BLK), jnp.float32),
            pltpu.VMEM((NOTE, BLK), jnp.bfloat16),
            pltpu.SemaphoreType.DMA((group + 1, 5)),
            pltpu.SemaphoreType.DMA,
            pltpu.SemaphoreType.DMA((group + 1, 4)),
        ],
        compiler_params=PARAMS,
        cost_estimate=pl.CostEstimate(
            flops=blocks * slots * 64 * BLK * BLK * HD,
            bytes_accessed=blocks * BLK * HD * 16,
            transcendentals=blocks * slots * BLK * BLK,
        ),
        name="attend",
    )(sink, sink_in, marks_in, *parcels, *extra)


def local(queries, keys, values, out_grad, adjacency, counts, sink):
    seq = lax.axis_size("seq")
    group = min(seq, GROUP)
    groups = seq // group
    heads = sink.shape[0]
    per_device = heads // group
    slots = adjacency.shape[2]
    own_blocks = adjacency.shape[1]
    span = own_blocks * BLK
    size = 4 * span
    halo = RADIUS * own_blocks if groups > 1 else 0
    scale = HD ** (-0.5)
    spot = lax.rem(lax.axis_index("seq"), group)

    def swap(x, k, axis="seq"):
        return lax.ppermute(x, axis, [(i, i ^ k) for i in range(lax.axis_size(axis))])

    def summed(x, axis, step, end):
        while step < end:
            x = x + swap(x, step, axis)
            step *= 2
        return x

    def beside(x, step):
        route = [(i, i + step * group) for i in range(seq) if 0 <= i + step * group < seq]
        return lax.ppermute(x, "seq", route)

    def halos(parcels, route):
        stacked = jnp.stack(
            [parcels[n][row * size : (row + 1) * size] for n, row in route["arrived"]]
        )
        ends = []
        for side, step in ((group - RADIUS, 1), (0, -1)):
            near = [stacked[(side + r) ^ spot] for r in range(RADIUS)]
            near = [jnp.concatenate([x[:span], x[span : 2 * span]], axis=1) for x in near]
            ends.append(beside(jnp.concatenate(near, axis=0), step))
        return jnp.stack(ends)

    def add_halos(results, halo_grads, route):
        stacked = jnp.stack(
            [results[n][row * size : (row + 1) * size] for n, row in route["sent"]]
        )
        for side, step, half in ((group - RADIUS, -1, 0), (0, 1, 1)):
            grads = beside(halo_grads[half], step)
            for r in range(RADIUS):
                at = (side + r) ^ spot
                rows = stacked[at]
                more = grads[r * span : (r + 1) * span]
                more = jnp.concatenate([more[:, :HD], more[:, HD:]], axis=0)
                wide = rows[: 2 * span].astype(jnp.float32) + more
                rows = jnp.concatenate([wide.astype(jnp.bfloat16), rows[2 * span :]], axis=0)
                stacked = lax.dynamic_update_index_in_dim(stacked, rows, at, 0)
        results = list(results)
        for k, (n, row) in enumerate(route["sent"]):
            results[n] = results[n].at[row * size : (row + 1) * size].set(stacked[k])
        return results

    constrained = [
        pltpu.with_memory_space_constraint(x, pltpu.HBM)
        for x in (adjacency, counts, keys, values, queries, out_grad)
    ]
    adjacency, counts, *sources = constrained
    shared = (adjacency, counts, sources)
    ahead = STEPS[1]
    items = [(0, k, 0, part) for k, (_, part) in enumerate(SWAP_AFTER["sent"]) if k // 2 * 2 == ahead]
    (soon,) = pack(*shared, [], items, SWAP_AFTER["sizes"][:1], 1, group, per_device)
    items = [
        (0, k, n - (n > 1), part)
        for k, (n, part) in enumerate(SWAP_AFTER["sent"])
        if k // 2 * 2 != ahead
    ]
    sizes = list(SWAP_AFTER["sizes"][:-1])
    noted = len(sizes)
    cross = len(SWAP_BEFORE["sizes"]) - 1
    sent = list(enumerate(SWAP_BEFORE["sent"]))
    for head in range(1, per_device):
        items += [(head, k, len(sizes), part) for k, (n, part) in sent if n == cross]
        sizes.append(SWAP_BEFORE["sizes"][cross])
    packed = list(pack(*shared, [soon], items, sizes, noted, group, per_device))
    filled = []
    for head in range(1, per_device):
        items = [(head, k, n, part) for k, (n, part) in sent if n != cross]
        own, *halves = pack(
            *shared, packed[:1], items, SWAP_BEFORE["sizes"][:cross], 0, group, per_device
        )
        crossed = swap(packed[noted + head - 1], 1)
        filled.append((own, merge(crossed, [], halves, size), crossed))
    between = SWAP_AFTER["steps"][1:]
    parcels = [packed[0]] + [swap(x, k) for x, k in zip([soon] + packed[1:noted], between)]
    awaited = [halves[0] for _, halves, _ in filled]
    first = split(parcels[:2], [], size, work=WORK)
    second = split(parcels[2:], [first] + awaited, size)
    arrived = [parcels + [swap(first, 1), swap(second, 1)]]
    routes_in = [SWAP_TWICE] + [SWAP_BEFORE] * (per_device - 1)
    for own, halves, crossed in filled:
        halves = after(arrived[-1][1:4], halves)
        arrived.append([own] + [swap(x, k) for x, k in zip(halves, between)] + [crossed])

    routes_out = [SWAP_AFTER] * (per_device - 1) + [SWAP_SOME]
    sink_row = jnp.zeros((1, BLK), jnp.float32)
    marks = jnp.zeros((own_blocks * group, HD), jnp.int32)
    before = arrived[-1][1:-1] if per_device > 1 else []
    returned = []
    for head in range(per_device):
        routes = (routes_in[head], routes_out[head])
        halo_in = halos(arrived[head], routes[0]) if halo else None
        done = attend(
            sink,
            sink_row,
            marks,
            arrived[head],
            halo_in,
            routes,
            group,
            per_device,
            head,
            halo,
            slots,
            own_blocks,
            scale,
        )
        count = len(routes[1]["sizes"])
        results, sink_row, marks = list(done[:count]), done[count], done[count + 1]
        if halo:
            results = add_halos(results, done[count + 2], routes[1])
        if before:
            results[1:] = after(before, results[1:])
        own, *halves = results
        steps = routes[1]["steps"][1:]
        if routes[1] is SWAP_SOME:
            crossed = swap(halves.pop(), 1)
            *halves[:2], sink_row = merge(crossed, [sink_row], halves[:2], size)
        before = [swap(x, k) for x, k in zip(halves, steps)]
        returned.append([own] + before)
    returned[-1].append(crossed)
    last = (routes_out[-1], span, group, per_device, per_device - 1)
    outs = unpack(returned[-1], (0, 3, 4), [], [], *last, work=WORK)
    sink_row = summed(sink_row, "dp", 1, lax.axis_size("dp"))
    sink_row = summed(sink_row, "seq", group, seq)
    for head in range(per_device - 1):
        parcels = returned[head] + [swap(split(returned[head], [crossed], size), 1)]
        *outs, sink_row = unpack(
            parcels, range(5), outs, [sink_row], routes_out[head], span, group, per_device, head
        )
    rows = [sink_row] + [swap(sink_row, k) for k in between]
    *outs, sink_grad = unpack(returned[-1], (1, 2, 5), outs, [], *last, rows=rows)
    value_grad, key_grad, attended, query_grad = outs
    return attended, query_grad, key_grad, value_grad, sink_grad


def solution(mesh):
    tokens = P("dp", "seq", None)
    return jax.shard_map(
        local,
        mesh=mesh,
        in_specs=(tokens, tokens, tokens, tokens, tokens, P("dp", "seq"), P()),
        out_specs=(tokens, tokens, tokens, tokens, P()),
        check_vma=False,
    )
```

```python
import functools

import jax
import jax.numpy as jnp
from jax import lax
from jax.experimental import pallas as pl
from jax.experimental.pallas import tpu as pltpu
from jax.sharding import PartitionSpec as P

HD = 128
BLK = 128
RADIUS = 2
GROUP = 8
NOTE = 16
WORK = 20_000_000_000
LOG2E = 1.4426950408889634
VMEM_LIMIT = 48 * 1024 * 1024
NT = (((1,), (1,)), ((), ()))
NN = (((1,), (0,)), ((), ()))
ANY = pl.BlockSpec(memory_space=pl.ANY)
SMEM = pl.BlockSpec(memory_space=pltpu.SMEM)
VMEM = pl.BlockSpec(memory_space=pltpu.VMEM)
PARAMS = pltpu.CompilerParams(vmem_limit_bytes=VMEM_LIMIT)


ORDER = (1, 2, 3)
STEPS = (0,) + tuple(2 * m for m in ORDER)
PLACE = {m: n for n, m in enumerate((0,) + ORDER)}
HALVES = tuple((PLACE[k // 2], k % 2) for k in range(GROUP))
SWAP_BEFORE = {
    "steps": STEPS + (1,),
    "sizes": (1, 2, 2, 2, 4),
    "sent": tuple((4, n) if e else (n, 0) for n, e in HALVES),
    "arrived_sizes": (1, 2, 2, 2, 4),
    "arrived": tuple((4, 0) if (n, e) == (0, 1) else (n, e) for n, e in HALVES),
}
SWAP_SOME = {
    "steps": (0, 4, 6, 2, 3, 1),
    "sizes": (1, 2, 2, 1, 1, 3),
    "sent": ((0, 0), (5, 0), (3, 0), (4, 0), (1, 0), (5, 1), (2, 0), (5, 2)),
    "arrived_sizes": (1, 2, 2, 1, 1, 3),
    "arrived": ((0, 0), (5, 0), (3, 0), (4, 0), (1, 0), (1, 1), (2, 0), (2, 1)),
}
SWAP_AFTER = {
    "steps": STEPS,
    "sizes": (2, 2, 2, 2),
    "sent": HALVES,
    "arrived_sizes": (2, 2, 2, 2, 4),
    "arrived": tuple((4, n) if e else (n, 0) for n, e in HALVES),
}
SWAP_TWICE = {
    "steps": STEPS,
    "sizes": (2, 2, 2, 2),
    "sent": HALVES,
    "arrived_sizes": (2, 2, 2, 2, 2, 2),
    "arrived": tuple((4 + n // 2, n % 2) if e else (n, 0) for n, e in HALVES),
}


def bytes_cost(count):
    return pl.CostEstimate(flops=0, bytes_accessed=count, transcendentals=0)


def run_copies(copies):
    for copy in copies:
        copy.start()
    for copy in copies:
        copy.wait()


def pack_kernel(group, per_device, tokens, items, noted, awaited, *refs):
    adjacency, counts = refs[:2]
    sources, outs = refs[2:6], refs[6 + awaited : -5]
    slots_here, counts_here, note, sems, list_sems = refs[-5:]
    rank = lax.axis_index("seq")
    spot = lax.rem(rank, group)
    copies = []
    for i, (head, k, n, row) in enumerate(items):
        column = pl.multiple_of(((spot ^ k) * per_device + head) * HD, HD)
        for a, source in enumerate(sources):
            copies.append(
                pltpu.make_async_copy(
                    source.at[0, :, pl.ds(column, HD)],
                    outs[n].at[pl.ds(row + a * tokens, tokens)],
                    sems.at[i, a],
                )
            )
    for copy in copies:
        copy.start()
    if noted:
        run_copies(
            (
                pltpu.make_async_copy(adjacency, slots_here, list_sems.at[0]),
                pltpu.make_async_copy(counts, counts_here, list_sems.at[1]),
            )
        )
        own_blocks, slots = adjacency.shape[1:]
        rows = lax.broadcasted_iota(jnp.int32, note.shape, 0)
        lanes = lax.broadcasted_iota(jnp.int32, note.shape, 1)
        marks = jnp.zeros(note.shape, jnp.int32)
        for b in range(own_blocks):
            for j in range(slots):
                near = slots_here[0, b, j] - rank * own_blocks
                marks = jnp.where((rows == b) & (lanes == j), near, marks)
            marks = jnp.where((rows == b) & (lanes == slots), counts_here[0, b], marks)
        note[...] = marks.astype(jnp.float32)
        for out in outs[:noted]:
            row = out.shape[0] // (4 * tokens) * 4 * tokens
            out[row : row + NOTE, :] = note[...].astype(jnp.bfloat16)
    for copy in copies:
        copy.wait()


def pack(adjacency, counts, sources, awaited, items, parts, noted, group, per_device):
    tokens = sources[0].shape[1]
    size = 4 * tokens
    items = [(head, k, n, part * size) for head, k, n, part in items]
    rows = [n * size + (NOTE if i < noted else 0) for i, n in enumerate(parts)]
    return pl.pallas_call(
        functools.partial(
            pack_kernel, group, per_device, tokens, items, noted, len(awaited)
        ),
        out_shape=[jax.ShapeDtypeStruct((r, HD), jnp.bfloat16) for r in rows],
        in_specs=[ANY] * (6 + len(awaited)),
        out_specs=[VMEM] * len(rows),
        scratch_shapes=[
            pltpu.SMEM(adjacency.shape, jnp.int32),
            pltpu.SMEM(counts.shape, jnp.int32),
            pltpu.VMEM((NOTE, HD), jnp.float32),
            pltpu.SemaphoreType.DMA((len(items), 4)),
            pltpu.SemaphoreType.DMA((2,)),
        ],
        compiler_params=PARAMS,
        cost_estimate=bytes_cost(len(items) * size * HD * 4),
        name="pack",
    )(adjacency, counts, *sources, *awaited)


def pass_kernel(*refs):
    pass


def after(awaited, arrays):
    return pl.pallas_call(
        pass_kernel,
        out_shape=[jax.ShapeDtypeStruct(x.shape, x.dtype) for x in arrays],
        in_specs=[ANY] * (len(arrays) + len(awaited)),
        out_specs=[ANY] * len(arrays),
        input_output_aliases={n: n for n in range(len(arrays))},
        compiler_params=PARAMS,
        cost_estimate=bytes_cost(0),
        name="after",
    )(*arrays, *awaited)


def split_kernel(pairs, size, noted, *refs):
    parcels, out, sems = refs[:pairs], refs[-2], refs[-1]
    copies = []
    for m in range(pairs):
        moves = [(size, m * size, size)]
        if noted:
            moves.append((2 * size, pairs * size + m * NOTE, NOTE))
        for i, (row, to, count) in enumerate(moves):
            copies.append(
                pltpu.make_async_copy(
                    parcels[m].at[pl.ds(row, count)], out.at[pl.ds(to, count)], sems.at[m, i]
                )
            )
    run_copies(copies)


def split(parcels, awaited, size, work=0):
    pairs = len(parcels)
    noted = parcels[0].shape[0] > 2 * size
    rows = pairs * (size + NOTE * noted)
    return pl.pallas_call(
        functools.partial(split_kernel, pairs, size, noted),
        out_shape=jax.ShapeDtypeStruct((rows, HD), jnp.bfloat16),
        in_specs=[ANY] * (pairs + len(awaited)),
        out_specs=VMEM,
        scratch_shapes=[pltpu.SemaphoreType.DMA((pairs, 2))],
        compiler_params=PARAMS,
        cost_estimate=pl.CostEstimate(
            flops=work, bytes_accessed=rows * HD * 4, transcendentals=0
        ),
        name="split",
    )(*parcels, *awaited)


def merge_kernel(size, count, noted, *refs):
    swapped, sems = refs[0], refs[-1]
    outs = refs[1 + count + noted : 1 + 2 * count + noted]
    if noted:
        rows = swapped[(count + 1) * size :, :].astype(jnp.float32)
        refs[-2][...] = refs[1][...] + jnp.sum(rows, axis=0, keepdims=True)
    run_copies(
        [
            pltpu.make_async_copy(
                swapped.at[pl.ds((n + 1) * size, size)], out.at[pl.ds(size, size)], sems.at[n]
            )
            for n, out in enumerate(outs)
        ]
    )


def merge(swapped, rows, halves, size):
    held = list(halves) + list(rows)
    return pl.pallas_call(
        functools.partial(merge_kernel, size, len(halves), len(rows)),
        out_shape=[jax.ShapeDtypeStruct(x.shape, x.dtype) for x in held],
        in_specs=[VMEM] * (1 + len(rows)) + [ANY] * len(halves),
        out_specs=[ANY] * len(halves) + [VMEM] * len(rows),
        scratch_shapes=[pltpu.SemaphoreType.DMA((len(halves),))],
        input_output_aliases={1 + len(rows) + n: n for n in range(len(halves))},
        compiler_params=PARAMS,
        cost_estimate=bytes_cost(len(halves) * size * HD * 4),
        name="merge",
    )(swapped, *rows, *halves)


def unpack_kernel(group, per_device, head, tokens, count, layout, passed, rows, *refs):
    parcels, sems = refs[:count], refs[-1]
    tail = passed + (rows > 0)
    outs = refs[-5 - tail : -1 - tail]
    if rows:
        total = functools.reduce(jnp.add, [row[...] for row in refs[count : count + rows]])
        refs[-2][...] = total[0, : group * per_device]
    spot = lax.rem(lax.axis_index("seq"), group)
    copies = []
    for i, (k, n, from_row) in enumerate(layout):
        column = pl.multiple_of(((spot ^ k) * per_device + head) * HD, HD)
        for a, out in enumerate(outs):
            copies.append(
                pltpu.make_async_copy(
                    parcels[n].at[pl.ds(from_row + a * tokens, tokens)],
                    out.at[0, :, pl.ds(column, HD)],
                    sems.at[i, a],
                )
            )
    run_copies(copies)


def unpack(parcels, which, outs, passed, route, tokens, group, per_device, head, work=0, rows=()):
    count = len(which)
    layout = [
        (k, which.index(n), row * 4 * tokens)
        for k, (n, row) in enumerate(route["arrived"])
        if n in which
    ]
    parcels = [parcels[n] for n in which]
    total = [jax.ShapeDtypeStruct((group * per_device,), jnp.float32)] if rows else []
    shape = jax.ShapeDtypeStruct((1, tokens, group * per_device * HD), jnp.bfloat16)
    return pl.pallas_call(
        functools.partial(
            unpack_kernel, group, per_device, head, tokens, count, layout, len(passed), len(rows)
        ),
        out_shape=[shape] * 4 + [jax.ShapeDtypeStruct(x.shape, x.dtype) for x in passed] + total,
        in_specs=[VMEM] * (count + len(rows)) + [ANY] * (len(outs) + len(passed)),
        out_specs=[ANY] * (4 + len(passed)) + [VMEM] * len(total),
        scratch_shapes=[pltpu.SemaphoreType.DMA((len(layout), 4))],
        input_output_aliases={
            count + len(rows) + n: 4 - len(outs) + n for n in range(len(outs) + len(passed))
        },
        compiler_params=PARAMS,
        cost_estimate=pl.CostEstimate(
            flops=work, bytes_accessed=len(layout) * tokens * HD * 16, transcendentals=0
        ),
        name="unpack",
    )(*parcels, *rows, *outs, *passed)


def attend_kernel(group, per_device, head, halo, slots, own_blocks, scale, route, *refs):
    sink, sink_in, marks_in = refs[:3]
    arriving, leaving = route
    count = len(arriving["arrived_sizes"])
    parcels, refs = refs[3 : 3 + count], refs[3 + count :]
    if halo:
        halo_in, refs = refs[0], refs[1:]
    count = len(leaving["sizes"])
    results, sink_out, marks = refs[:count], refs[count], refs[count + 1]
    refs = refs[count + 2 :]
    if halo:
        halo_out, refs = refs[0], refs[1:]
    kv, qd, notes, lists, kt, vt, diag, diag_back, scored, paired, acc, out = refs[:12]
    sink_acc, sink_note, sems, list_sem, out_sems = refs[12:]

    blocks = own_blocks * group
    span = own_blocks * BLK
    edge = halo * BLK
    window = blocks + 2 * halo
    spot = lax.rem(lax.axis_index("seq"), group)
    number = spot * per_device + head
    note_copies, copies = [], []
    for k, (n, row) in enumerate(arriving["arrived"] if head == 0 else ()):
        row = arriving["arrived_sizes"][n] * 4 * span + row * NOTE
        note_copies.append(
            pltpu.make_async_copy(
                parcels[n].at[pl.ds(row, NOTE)], notes.at[spot ^ k], sems.at[k, 4]
            )
        )
    for k in range(group):
        row = pl.multiple_of((spot ^ k) * span, span)
        targets = (
            kv.at[pl.ds(row + edge, span), pl.ds(0, HD)],
            kv.at[pl.ds(row + edge, span), pl.ds(HD, HD)],
            qd.at[pl.ds(row, span), pl.ds(0, HD)],
            qd.at[pl.ds(row, span), pl.ds(HD, HD)],
        )
        n, part = arriving["arrived"][k]
        from_row = part * 4 * span
        for a, target in enumerate(targets):
            copies.append(
                pltpu.make_async_copy(
                    parcels[n].at[pl.ds(from_row + a * span, span)], target, sems.at[k, a]
                )
            )
    if halo:
        copies.append(pltpu.make_async_copy(halo_in.at[0], kv.at[pl.ds(0, edge)], sems.at[group, 0]))
        copies.append(
            pltpu.make_async_copy(
                halo_in.at[1], kv.at[pl.ds(edge + blocks * BLK, edge)], sems.at[group, 1]
            )
        )
    for copy in note_copies + copies:
        copy.start()
    diag[...] = jnp.zeros_like(diag)
    diag_back[...] = jnp.zeros_like(diag_back)
    acc[...] = jnp.zeros_like(acc)
    sink_acc[...] = jnp.zeros_like(sink_acc)
    for copy in note_copies:
        copy.wait()
    if head == 0:
        for j in range(group):
            marks[pl.ds(j * own_blocks, own_blocks), :] = (
                notes[j].astype(jnp.float32).astype(jnp.int32)[:own_blocks]
            )
    else:
        marks[...] = marks_in[...]
    list_copy = pltpu.make_async_copy(marks, lists, list_sem)
    list_copy.start()
    for copy in copies:
        copy.wait()

    def turn(c, carry):
        rows = kv[pl.ds(pl.multiple_of(c * BLK, BLK), BLK), :]
        kt[c] = rows[:, :HD].T
        vt[c] = rows[:, HD:].T
        return carry

    lax.fori_loop(0, window, turn, 0)
    list_copy.wait()

    to_log2 = scale * LOG2E
    sink_log2 = sink[number] * LOG2E

    def folded(x, op):
        return functools.reduce(op, [x[r : r + 8] for r in range(0, x.shape[0], 8)])

    def one_block(b, carry):
        rows = pl.ds(pl.multiple_of(b * BLK, BLK), BLK)
        home = b // own_blocks * own_blocks + halo
        query = qd[rows, :HD]
        grad = qd[rows, HD:]
        diag[:BLK, :HD] = query
        diag[BLK:, HD:] = grad
        diag_back[:BLK, :HD] = grad
        diag_back[BLK:, HD:] = query

        def with_slots(live):
            at = [lists[b, j] + home for j in range(live)]
            key_rows = [pl.ds(pl.multiple_of(c * BLK, BLK), BLK) for c in at]
            weights = diag[...]
            top = None
            for j in range(live):
                both = lax.dot_general(kv[key_rows[j], :], weights, NT, preferred_element_type=jnp.float32)
                scored[j] = both
                part = folded(both[:, :BLK], jnp.maximum)
                top = part if top is None else jnp.maximum(top, part)
            top = jnp.maximum(jnp.max(top, axis=0, keepdims=True) * to_log2, sink_log2)
            total = jnp.zeros((8, BLK), jnp.float32)
            dotted = jnp.zeros((8, BLK), jnp.float32)
            for j in range(live):
                power = jnp.exp2(scored[j, :, :BLK] * to_log2 - top)
                scored[j, :, :BLK] = power
                total = total + folded(power, jnp.add)
                dotted = dotted + folded(power * scored[j, :, BLK:], jnp.add)
            sink_power = jnp.exp2(sink_log2 - top)
            inverse = 1.0 / (jnp.sum(total, axis=0, keepdims=True) + sink_power)
            delta = jnp.sum(dotted, axis=0, keepdims=True) * inverse
            sink_acc[...] += sink_power * inverse * delta
            weights = diag_back[...]
            for j in range(live):
                probs = scored[j, :, :BLK] * inverse
                dscores = probs * (scored[j, :, BLK:] - delta)
                pair = jnp.concatenate([probs, dscores], axis=1).astype(jnp.bfloat16)
                paired[pl.ds(j * BLK, BLK), :] = pair
                acc[key_rows[j], :] += lax.dot_general(
                    pair, weights, NN, preferred_element_type=jnp.float32
                )
            attended = lax.dot_general(
                jnp.concatenate([vt[c] for c in at], axis=1),
                paired[: live * BLK, :BLK],
                NN,
                preferred_element_type=jnp.float32,
            )
            query_grad = lax.dot_general(
                jnp.concatenate([kt[c] for c in at], axis=1),
                paired[: live * BLK, BLK:],
                NN,
                preferred_element_type=jnp.float32,
            )
            out[2, rows, :] = attended.astype(jnp.bfloat16).T
            out[3, rows, :] = (query_grad * scale).astype(jnp.bfloat16).T

        for live in range(1, slots + 1):
            pl.when(lists[b, slots] == live)(functools.partial(with_slots, live))
        return carry

    lax.fori_loop(0, blocks, one_block, 0)

    def finish(b, carry):
        rows = pl.ds(pl.multiple_of(b * BLK, BLK), BLK)
        from_rows = pl.ds(pl.multiple_of((b + halo) * BLK, BLK), BLK)
        out[0, rows, :] = acc[from_rows, :HD].astype(jnp.bfloat16)
        out[1, rows, :] = (acc[from_rows, HD:] * scale).astype(jnp.bfloat16)
        return carry

    lax.fori_loop(0, blocks, finish, 0)
    lanes = lax.broadcasted_iota(jnp.int32, (1, BLK), 1)
    sink_sum = jnp.sum(sink_acc[...], axis=1, keepdims=True)
    sink_row = sink_in[...] - jnp.where(lanes == number, sink_sum, 0.0)
    sink_out[...] = sink_row
    copies = []
    if leaving is SWAP_SOME:
        lines = lax.broadcasted_iota(jnp.int32, (NOTE, BLK), 0)
        rest, rows = sink_row, jnp.zeros((NOTE, BLK), jnp.float32)
        for line in range(3):
            piece = rest.astype(jnp.bfloat16).astype(jnp.float32)
            rows = jnp.where(lines == line, piece, rows)
            rest = rest - piece
        sink_note[...] = rows.astype(jnp.bfloat16)
        room = results[-1].at[pl.ds(leaving["sizes"][-1] * 4 * span, NOTE)]
        copies.append(pltpu.make_async_copy(sink_note, room, out_sems.at[group, 0]))
    for k in range(group):
        row = pl.multiple_of((spot ^ k) * span, span)
        n, part = leaving["sent"][k]
        to_row = part * 4 * span
        for a in range(4):
            copies.append(
                pltpu.make_async_copy(
                    out.at[a, pl.ds(row, span)],
                    results[n].at[pl.ds(to_row + a * span, span)],
                    out_sems.at[k, a],
                )
            )
    for copy in copies:
        copy.start()
    if halo:
        for side, row in ((0, 0), (1, edge + blocks * BLK)):
            halo_out[side, :, :HD] = acc[pl.ds(row, edge), :HD]
            halo_out[side, :, HD:] = acc[pl.ds(row, edge), HD:] * scale
    for copy in copies:
        copy.wait()


def attend(sink, sink_in, marks_in, parcels, halo_in, routes, group, per_device, head, halo, slots, own_blocks, scale):
    span = own_blocks * BLK
    edge = halo * BLK
    blocks = own_blocks * group
    window = blocks + 2 * halo
    rows = [n * 4 * span for n in routes[1]["sizes"]]
    if routes[1] is SWAP_SOME:
        rows[-1] += NOTE
    out_shape = [jax.ShapeDtypeStruct((n, HD), jnp.bfloat16) for n in rows]
    out_specs = [ANY] * len(out_shape) + [VMEM] * 2
    out_shape.append(jax.ShapeDtypeStruct((1, BLK), jnp.float32))
    out_shape.append(jax.ShapeDtypeStruct((blocks, HD), jnp.int32))
    extra = []
    if halo:
        extra = [halo_in]
        out_shape.append(jax.ShapeDtypeStruct((2, edge, 2 * HD), jnp.float32))
        out_specs.append(VMEM)
    return pl.pallas_call(
        functools.partial(
            attend_kernel, group, per_device, head, halo, slots, own_blocks, scale, routes
        ),
        out_shape=out_shape,
        in_specs=[SMEM, VMEM, VMEM] + [ANY] * (len(parcels) + len(extra)),
        out_specs=out_specs,
        scratch_shapes=[
            pltpu.VMEM((window * BLK, 2 * HD), jnp.bfloat16),
            pltpu.VMEM((blocks * BLK, 2 * HD), jnp.bfloat16),
            pltpu.VMEM((group, NOTE, HD), jnp.bfloat16),
            pltpu.SMEM((blocks, HD), jnp.int32),
            pltpu.VMEM((window, HD, BLK), jnp.bfloat16),
            pltpu.VMEM((window, HD, BLK), jnp.bfloat16),
            pltpu.VMEM((2 * BLK, 2 * HD), jnp.bfloat16),
            pltpu.VMEM((2 * BLK, 2 * HD), jnp.bfloat16),
            pltpu.VMEM((slots, BLK, 2 * BLK), jnp.float32),
            pltpu.VMEM((slots * BLK, 2 * BLK), jnp.bfloat16),
            pltpu.VMEM((window * BLK, 2 * HD), jnp.float32),
            pltpu.VMEM((4, blocks * BLK, HD), jnp.bfloat16),
            pltpu.VMEM((1, BLK), jnp.float32),
            pltpu.VMEM((NOTE, BLK), jnp.bfloat16),
            pltpu.SemaphoreType.DMA((group + 1, 5)),
            pltpu.SemaphoreType.DMA,
            pltpu.SemaphoreType.DMA((group + 1, 4)),
        ],
        compiler_params=PARAMS,
        cost_estimate=pl.CostEstimate(
            flops=blocks * slots * 64 * BLK * BLK * HD,
            bytes_accessed=blocks * BLK * HD * 16,
            transcendentals=blocks * slots * BLK * BLK,
        ),
        name="attend",
    )(sink, sink_in, marks_in, *parcels, *extra)


def local(queries, keys, values, out_grad, adjacency, counts, sink):
    seq = lax.axis_size("seq")
    group = min(seq, GROUP)
    groups = seq // group
    heads = sink.shape[0]
    per_device = heads // group
    slots = adjacency.shape[2]
    own_blocks = adjacency.shape[1]
    span = own_blocks * BLK
    size = 4 * span
    halo = RADIUS * own_blocks if groups > 1 else 0
    scale = HD ** (-0.5)
    spot = lax.rem(lax.axis_index("seq"), group)

    def swap(x, k, axis="seq"):
        return lax.ppermute(x, axis, [(i, i ^ k) for i in range(lax.axis_size(axis))])

    def summed(x, axis, step, end):
        while step < end:
            x = x + swap(x, step, axis)
            step *= 2
        return x

    def beside(x, step):
        route = [(i, i + step * group) for i in range(seq) if 0 <= i + step * group < seq]
        return lax.ppermute(x, "seq", route)

    def halos(parcels, route):
        stacked = jnp.stack(
            [parcels[n][row * size : (row + 1) * size] for n, row in route["arrived"]]
        )
        ends = []
        for side, step in ((group - RADIUS, 1), (0, -1)):
            near = [stacked[(side + r) ^ spot] for r in range(RADIUS)]
            near = [jnp.concatenate([x[:span], x[span : 2 * span]], axis=1) for x in near]
            ends.append(beside(jnp.concatenate(near, axis=0), step))
        return jnp.stack(ends)

    def add_halos(results, halo_grads, route):
        stacked = jnp.stack(
            [results[n][row * size : (row + 1) * size] for n, row in route["sent"]]
        )
        for side, step, half in ((group - RADIUS, -1, 0), (0, 1, 1)):
            grads = beside(halo_grads[half], step)
            for r in range(RADIUS):
                at = (side + r) ^ spot
                rows = stacked[at]
                more = grads[r * span : (r + 1) * span]
                more = jnp.concatenate([more[:, :HD], more[:, HD:]], axis=0)
                wide = rows[: 2 * span].astype(jnp.float32) + more
                rows = jnp.concatenate([wide.astype(jnp.bfloat16), rows[2 * span :]], axis=0)
                stacked = lax.dynamic_update_index_in_dim(stacked, rows, at, 0)
        results = list(results)
        for k, (n, row) in enumerate(route["sent"]):
            results[n] = results[n].at[row * size : (row + 1) * size].set(stacked[k])
        return results

    constrained = [
        pltpu.with_memory_space_constraint(x, pltpu.HBM)
        for x in (adjacency, counts, keys, values, queries, out_grad)
    ]
    adjacency, counts, *sources = constrained
    shared = (adjacency, counts, sources)
    ahead = STEPS[1]
    items = [(0, k, 0, part) for k, (_, part) in enumerate(SWAP_AFTER["sent"]) if k // 2 * 2 == ahead]
    (soon,) = pack(*shared, [], items, SWAP_AFTER["sizes"][:1], 1, group, per_device)
    items = [
        (0, k, n - (n > 1), part)
        for k, (n, part) in enumerate(SWAP_AFTER["sent"])
        if k // 2 * 2 != ahead
    ]
    sizes = list(SWAP_AFTER["sizes"][:-1])
    noted = len(sizes)
    cross = len(SWAP_BEFORE["sizes"]) - 1
    sent = list(enumerate(SWAP_BEFORE["sent"]))
    for head in range(1, per_device):
        items += [(head, k, len(sizes), part) for k, (n, part) in sent if n == cross]
        sizes.append(SWAP_BEFORE["sizes"][cross])
    packed = list(pack(*shared, [soon], items, sizes, noted, group, per_device))
    filled = []
    for head in range(1, per_device):
        items = [(head, k, n, part) for k, (n, part) in sent if n != cross]
        own, *halves = pack(
            *shared, packed[:1], items, SWAP_BEFORE["sizes"][:cross], 0, group, per_device
        )
        crossed = swap(packed[noted + head - 1], 1)
        filled.append((own, merge(crossed, [], halves, size), crossed))
    between = SWAP_AFTER["steps"][1:]
    parcels = [packed[0]] + [swap(x, k) for x, k in zip([soon] + packed[1:noted], between)]
    awaited = [halves[0] for _, halves, _ in filled]
    first = split(parcels[:2], [], size, work=WORK)
    second = split(parcels[2:], [first] + awaited, size)
    arrived = [parcels + [swap(first, 1), swap(second, 1)]]
    routes_in = [SWAP_TWICE] + [SWAP_BEFORE] * (per_device - 1)
    for own, halves, crossed in filled:
        halves = after(arrived[-1][1:4], halves)
        arrived.append([own] + [swap(x, k) for x, k in zip(halves, between)] + [crossed])

    routes_out = [SWAP_AFTER] * (per_device - 1) + [SWAP_SOME]
    sink_row = jnp.zeros((1, BLK), jnp.float32)
    marks = jnp.zeros((own_blocks * group, HD), jnp.int32)
    before = arrived[-1][1:-1] if per_device > 1 else []
    returned = []
    for head in range(per_device):
        routes = (routes_in[head], routes_out[head])
        halo_in = halos(arrived[head], routes[0]) if halo else None
        done = attend(
            sink,
            sink_row,
            marks,
            arrived[head],
            halo_in,
            routes,
            group,
            per_device,
            head,
            halo,
            slots,
            own_blocks,
            scale,
        )
        count = len(routes[1]["sizes"])
        results, sink_row, marks = list(done[:count]), done[count], done[count + 1]
        if halo:
            results = add_halos(results, done[count + 2], routes[1])
        if before and head < per_device - 1:
            results[1:2] = after(before[:1], results[1:2])
            results[2:] = after(before[1:] + results[1:2], results[2:])
        elif before:
            results[1:] = after(before, results[1:])
        own, *halves = results
        steps = routes[1]["steps"][1:]
        if routes[1] is SWAP_SOME:
            crossed = swap(halves.pop(), 1)
            *halves[:2], sink_row = merge(crossed, [sink_row], halves[:2], size)
        before = [swap(x, k) for x, k in zip(halves, steps)]
        returned.append([own] + before)
    returned[-1].append(crossed)
    last = (routes_out[-1], span, group, per_device, per_device - 1)
    outs = unpack(returned[-1], (0, 3, 4), [], [], *last, work=WORK)
    sink_row = summed(sink_row, "dp", 1, lax.axis_size("dp"))
    sink_row = summed(sink_row, "seq", group, seq)
    for head in range(per_device - 1):
        parcels = returned[head] + [swap(split(returned[head], [crossed], size), 1)]
        *outs, sink_row = unpack(
            parcels, range(5), outs, [sink_row], routes_out[head], span, group, per_device, head
        )
    rows = [sink_row] + [swap(sink_row, k) for k in between]
    *outs, sink_grad = unpack(returned[-1], (1, 2, 5), outs, [], *last, rows=rows)
    value_grad, key_grad, attended, query_grad = outs
    return attended, query_grad, key_grad, value_grad, sink_grad


def solution(mesh):
    tokens = P("dp", "seq", None)
    return jax.shard_map(
        local,
        mesh=mesh,
        in_specs=(tokens, tokens, tokens, tokens, tokens, P("dp", "seq"), P()),
        out_specs=(tokens, tokens, tokens, tokens, P()),
        check_vma=False,
    )
```
